256 devices in a mesh: dp: 8 (over y, core), expert: 32 (over z, x).
Axes of the slice: x: 4, y: 4, z: 8, core: 2. Of those that a mesh axis runs over, the one named last changes fastest.
Arguments:
- tokens: bfloat16 [32768, 1280], P(('dp', 'expert')), may hold values from -6 to 6
- grad_out: bfloat16 [32768, 1280], P(('dp', 'expert')), may hold values from -6 to 6
- gate: bfloat16 [32768], P(('dp', 'expert')), may hold values from 0.19921875 to 1
- expert_ids: int32 [32768, 1], P(('dp', 'expert')), may hold values from 0 to 31; in each aligned block of 128 rows (0 to 127, 128 to 255, ...) at most 6 rows name the same one
- modality: int32 [32768], P(('dp', 'expert')), may hold values 0 or 1
- modal_gain: float32 [2, 1280], replicated, may hold values from 0.5 to 2
- w_in: bfloat16 [32, 1280, 5120], P('expert', None, 'dp'), may hold values from -0.15625 to 0.15625
- w_out: bfloat16 [32, 5120, 1280], P('expert', 'dp'), may hold values from -0.078125 to 0.078125
Outputs:
- grad_tokens: bfloat16 [32768, 1280], P(('dp', 'expert'))
- grad_gate: bfloat16 [32768], P(('dp', 'expert'))
- grad_w_in: bfloat16 [32, 1280, 5120], P('expert', None, 'dp')
- grad_w_out: bfloat16 [32, 5120, 1280], P('expert', 'dp')
The draws below stay inside these ranges and needn't reach their ends.
Inputs may be any that keep to these rules, and one draw needn't show every extreme that they name: `expert_ids`: in each aligned block of 128 tokens (the tokens of one device) no expert is named more than 6 times, a bound that some block reaches.
All inputs are finite; a program needn't handle non-finite values. No bound on the sum of `modality` on one device may be relied on, other than what follows from the above.
Results may differ from the reference program's by a relative error of at most 0.017.
Values may be sent and summed in bfloat16 or wider, within the bound.
A program may use at most 128 MiB of HBM per device.

```python
import math
import jax
import jax.numpy as jnp
import numpy as np
from jax import lax

D = 1280
FF = 5120
TOK_DEV = 128
EXPERTS = 32
TOKENS = 32768
CAP = 6
FFS = 640
ROWS = 1536
N_DP = 8
N_EXPERT = 32


def with_ends(result, key, smallest, high):
    dims = result.shape
    spot = [jax.random.randint(jax.random.fold_in(key, axis), (), 0, dims[axis]) for axis in range(len(dims))]
    result = result.at[tuple(spot)].set(smallest)
    longest = dims.index(max(dims))
    spot[longest] = (spot[longest] + 1) % dims[longest]
    return result.at[tuple(spot)].set(high)


def steps_of(own_key, extent, pieces, smallest, top_value):
    factor_of, own = 1.0, jax.random.fold_in(own_key, 6)
    for dim, shards_of in pieces:
        heights = jnp.exp(jax.random.uniform(jax.random.fold_in(own, dim), (shards_of,), jnp.float32, smallest / len(pieces), top_value / len(pieces)))
        factor_of = factor_of * jnp.repeat(heights, extent[dim] // shards_of).reshape([-1 if axis == dim else 1 for axis in range(len(extent))])
    return factor_of


def routed_block(stream_key, own, number, rows, number_of, top, limit, skew):
    ranking = jax.random.permutation(stream_key, number_of)
    heavy_load, common = shares(number_of, rows * top, limit, skew, True), shares(number_of, rows * top, limit, skew, False)
    places = jnp.arange(number_of)

    def named(lengths, turn):
        used = int((lengths > 0).sum())
        fixed = max(1, used // 4)
        moved = fixed + (places - fixed + turn * (used - fixed)) % max(1, number_of - fixed)
        return jnp.zeros((number_of,), jnp.int32).at[ranking[jnp.where(places < fixed, places, moved)]].set(jnp.asarray(lengths, jnp.int32))

    lengths = jnp.where(number % 4 == 0, named(heavy_load, number // 4), named(common, number - number // 4 - 1))
    mixed = jax.random.permutation(jax.random.fold_in(own, 3), number_of)
    source_of, receiver = mixed[0:number_of // 2 * 2:2], mixed[1:number_of // 2 * 2:2]
    margin = jnp.minimum(lengths[source_of] - 1, limit - lengths[receiver]) // 2
    margin = jnp.where((source_of == ranking[0]) | (receiver == ranking[0]) | (lengths[receiver] == 0), 0, jnp.maximum(margin, 0))
    moved = jax.random.randint(jax.random.fold_in(own, 4), (number_of // 2,), 0, 1 << 20) % (margin + 1)
    lengths = lengths.at[source_of].add(-moved).at[receiver].add(moved)
    members = jnp.searchsorted(jnp.cumsum(lengths), jnp.arange(rows * top), side="right").astype(jnp.int32)
    grid = members.reshape(top, rows).T
    grid = grid[jax.random.permutation(jax.random.fold_in(own, 1), rows)]
    turn = jax.random.randint(jax.random.fold_in(own, 2), (rows, 1), 0, top)
    return jnp.take_along_axis(grid, (jnp.arange(top)[None, :] + turn) % top, axis=1)


def shares(amount, total, bound, skew, full):
    portions = [(1 << 20) // math.isqrt(standing ** skew) + 1 for standing in range(1, amount + 1)]
    largest = bound if full else min(bound, max(-(-total // amount), total * portions[0] // sum(portions)))
    least = 1 if total - largest >= amount - 1 else 0
    given, surplus = [largest] + [least] * (amount - 1), total - largest - least * (amount - 1)
    while surplus > 0:
        candidates = [i for i in range(1, amount) if given[i] < largest] or [i for i in range(1, amount) if given[i] < bound]
        pool, budget = sum([portions[i] for i in candidates]), surplus
        for i in candidates:
            extra = min(bound - given[i], max(1, budget * portions[i] // pool), surplus)
            given[i] = given[i] + extra
            surplus = surplus - extra
    return np.array(given)


def centred(own_key, dims, spread, bound, cuts=(), kind=jnp.bfloat16):
    values = jax.random.normal(own_key, dims, jnp.float32) * spread
    if len(cuts) > 0:
        values = steps_of(own_key, dims, cuts, -0.22, 0.18) * values
    return jnp.clip(values, min=-bound, max=bound).astype(kind)


def setup_inputs(seed: int = 0) -> dict:
    keys = jax.random.split(jax.random.key(seed), 9)
    tokens = centred(keys[0], (TOKENS, D), 1.0, 6.0, ((0, 256),))
    grad_out = centred(keys[1], (TOKENS, D), 1.0, 6.0, ((0, 256),))
    gate = jnp.clip(0.19921875 + 0.80078125 * jax.random.uniform(keys[2], (TOKENS,), jnp.float32) ** steps_of(keys[2], (TOKENS,), ((0, 256),), -0.2, 0.2), 0.19921875, 1.0).astype(jnp.bfloat16)
    expert_ids_keys = jax.random.split(jax.random.fold_in(keys[3], 1), TOKENS // TOK_DEV)
    expert_ids_turns = jax.random.permutation(jax.random.fold_in(keys[3], 3), TOKENS // TOK_DEV)
    expert_ids = jax.vmap(lambda own, number: routed_block(jax.random.fold_in(keys[3], 2), own, number, TOK_DEV, EXPERTS, 1, CAP, 2))(expert_ids_keys, expert_ids_turns).reshape((TOKENS, 1))
    modality = with_ends((jax.random.randint(keys[4], (TOKENS,), 0, 4) < 1).astype(jnp.int32), jax.random.fold_in(keys[4], 1), 0, 1)
    modal_gain = jnp.clip(jnp.exp(jax.random.uniform(keys[5], (2, D), jnp.float32, math.log(0.5), math.log(2.0))), 0.5, 2.0)
    w_in = centred(keys[6], (EXPERTS, D, FF), D ** -0.5, 0.15625, ((0, 32), (2, 8)))
    w_out = centred(keys[7], (EXPERTS, FF, D), FF ** -0.5, 0.078125, ((0, 32), (1, 8)))
    return dict(tokens=tokens, grad_out=grad_out, gate=gate, expert_ids=expert_ids, modality=modality, modal_gain=modal_gain, w_in=w_in, w_out=w_out)


inv_root_two = 0.7071067811865476
inv_root_two_pi = 0.3989422804014327


def gelu_parts(pre_act):
    normal_cdf = 0.5 * (1.0 + jax.scipy.special.erf(pre_act * inv_root_two))
    density = jnp.exp(-0.5 * pre_act * pre_act) * inv_root_two_pi
    return pre_act * normal_cdf, normal_cdf + pre_act * density


def reference(tokens, grad_out, gate, expert_ids, modality, modal_gain, w_in, w_out):
    chosen = expert_ids[:, 0]
    gain_rows = jnp.where(modality[:, None] == 1, modal_gain[1][None, :], modal_gain[0][None, :])
    scaled = (gain_rows * grad_out.astype(jnp.float32)).astype(jnp.bfloat16)
    by_expert = jnp.argsort(chosen, stable=True).astype(jnp.int32)
    expert_iota = jnp.arange(N_EXPERT, dtype=jnp.int32)
    counts = jnp.sum((chosen[None, :] == expert_iota[:, None]).astype(jnp.int32), axis=1)
    starts = jnp.cumsum(counts) - counts
    rows_iota = jnp.arange(ROWS, dtype=jnp.int32)

    def one_expert(expert):
        index_rows = jnp.minimum(starts[expert] + rows_iota, TOKENS - 1).astype(jnp.int32)
        live_rows = rows_iota < counts[expert]
        picked = by_expert[index_rows]
        rows_in = jnp.where(live_rows[:, None], tokens[picked], jnp.zeros((), jnp.bfloat16))
        rows_grad = jnp.where(live_rows[:, None], scaled[picked], jnp.zeros((), jnp.bfloat16))
        rows_gate = jnp.where(live_rows, gate[picked].astype(jnp.float32), jnp.float32(0.0))
        weight_in = w_in[expert]
        weight_out = w_out[expert]
        pre_act = jnp.dot(rows_in, weight_in, preferred_element_type=jnp.float32)
        activation, slope = gelu_parts(pre_act)
        held_act = (rows_gate[:, None] * activation).astype(jnp.bfloat16)
        out_grads = jnp.dot(held_act.T, rows_grad, preferred_element_type=jnp.float32).astype(jnp.bfloat16)
        back_grad = jnp.dot(rows_grad, weight_out.T, preferred_element_type=jnp.float32)
        pre_grad = (rows_gate[:, None] * back_grad * slope).astype(jnp.bfloat16)
        in_grads = jnp.dot(rows_in.T, pre_grad, preferred_element_type=jnp.float32).astype(jnp.bfloat16)
        grouped = pre_grad.astype(jnp.float32).reshape(ROWS, N_DP, FFS)
        weight_groups = weight_in.astype(jnp.float32).reshape(D, N_DP, FFS)
        token_parts = jnp.einsum('rgk,dgk->grd', grouped, weight_groups)
        token_parts = lax.optimization_barrier(token_parts.astype(jnp.bfloat16))
        token_total = jnp.sum(token_parts.astype(jnp.float32), axis=0)
        gate_parts = jnp.sum((activation * back_grad).reshape(ROWS, N_DP, FFS), axis=2)
        gate_parts = lax.optimization_barrier(gate_parts.astype(jnp.bfloat16))
        gate_total = jnp.sum(gate_parts.astype(jnp.float32), axis=1)
        token_total = jnp.where(live_rows[:, None], token_total, jnp.float32(0.0))
        gate_total = jnp.where(live_rows, gate_total, jnp.float32(0.0))
        return in_grads, out_grads, token_total, gate_total, picked

    in_all, out_all, token_all, gate_all, picked_all = lax.map(one_expert, expert_iota)
    flat_picked = picked_all.reshape(-1)
    grad_tokens = jnp.zeros((TOKENS, D), jnp.float32).at[flat_picked].add(token_all.reshape(-1, D))
    grad_gate = jnp.zeros((TOKENS,), jnp.float32).at[flat_picked].add(gate_all.reshape(-1))
    return grad_tokens.astype(jnp.bfloat16), grad_gate.astype(jnp.bfloat16), in_all, out_all
```

```python
import jax
import jax.numpy as jnp
from jax import lax
from jax.sharding import PartitionSpec as P

inv_root_two = 0.7071067811865476
inv_root_two_pi = 0.3989422804014327


def gelu_parts(pre_act):
    normal_cdf = 0.5 * (1.0 + lax.erf(pre_act * inv_root_two))
    density = jnp.exp(-0.5 * pre_act * pre_act) * inv_root_two_pi
    return (pre_act * normal_cdf, normal_cdf + pre_act * density)


def local(tokens, grad_out, gate, expert_ids, modality, modal_gain, w_in, w_out):
    experts = lax.axis_size("expert")
    tok_rows, width = tokens.shape
    cap = 3 * tok_rows // (2 * experts)
    chosen = expert_ids[:, 0]
    ids = jnp.arange(tok_rows, dtype=jnp.int32)
    same = (chosen[:, None] == chosen[None, :]) & (ids[None, :] < ids[:, None])
    slot_pos = jnp.sum(same.astype(jnp.int32), axis=1)
    target = chosen * cap + slot_pos
    select = (jnp.arange(experts * cap, dtype=jnp.int32)[:, None] == target[None, :]).astype(jnp.bfloat16)
    gate_wide = gate.astype(jnp.float32)
    gain_rows = jnp.where(modality[:, None] == 1, modal_gain[1][None, :], modal_gain[0][None, :])
    gated = (gate_wide[:, None] * gain_rows * grad_out.astype(jnp.float32)).astype(jnp.bfloat16)
    both = jnp.concatenate([tokens, gated], axis=1)
    send = jnp.dot(select, both, preferred_element_type=jnp.float32).astype(jnp.bfloat16)
    got = lax.all_to_all(send.reshape(experts, cap, 2 * width), "expert", split_axis=0, concat_axis=0, tiled=True)
    rows = lax.all_gather(got.reshape(experts * cap, 2 * width), "dp", axis=0, tiled=True)
    rows_in, rows_grad = rows[:, :width], rows[:, width:]
    weight_in, weight_out = w_in[0], w_out[0]
    pre_act = jnp.dot(rows_in, weight_in, preferred_element_type=jnp.float32)
    activation, slope = gelu_parts(pre_act)
    back_grad = lax.dot_general(rows_grad, weight_out, (((1,), (1,)), ((), ())), preferred_element_type=jnp.float32)
    gate_part = jnp.sum(activation * back_grad, axis=1)
    pre_grad = (back_grad * slope).astype(jnp.bfloat16)
    token_part = lax.dot_general(pre_grad, weight_in, (((1,), (1,)), ((), ())), preferred_element_type=jnp.float32)
    parts = jnp.concatenate(
        [token_part.astype(jnp.bfloat16), jnp.broadcast_to(gate_part.astype(jnp.bfloat16)[:, None], (rows.shape[0], 128))],
        axis=1,
    )
    summed = lax.psum_scatter(parts, "dp", scatter_dimension=0, tiled=True)
    home = lax.all_to_all(
        summed.reshape(experts, cap, width + 128), "expert", split_axis=0, concat_axis=0, tiled=True
    ).reshape(experts * cap, width + 128)
    out_grads = lax.dot_general(
        activation.astype(jnp.bfloat16), rows_grad, (((0,), (0,)), ((), ())), preferred_element_type=jnp.float32
    )
    in_grads = lax.dot_general(rows_in, pre_grad, (((0,), (0,)), ((), ())), preferred_element_type=jnp.float32)
    result = lax.dot_general(select, home, (((0,), (0,)), ((), ())), preferred_element_type=jnp.float32)
    return (
        result[:, :width].astype(jnp.bfloat16),
        (result[:, width] / gate_wide).astype(jnp.bfloat16),
        in_grads.astype(jnp.bfloat16)[None],
        out_grads.astype(jnp.bfloat16)[None],
    )


def solution(mesh):
    rows = P(("dp", "expert"), None)
    flat = P(("dp", "expert"))
    return jax.shard_map(
        local,
        mesh=mesh,
        in_specs=(rows, rows, flat, rows, flat, P(), P("expert", None, "dp"), P("expert", "dp", None)),
        out_specs=(rows, flat, P("expert", None, "dp"), P("expert", "dp", None)),
        check_vma=False,
    )
```

```python
import functools

import jax
import jax.numpy as jnp
from jax import lax
from jax.experimental import pallas as pl
from jax.experimental.pallas import tpu as pltpu
from jax.sharding import PartitionSpec as P

MESH = pl.DeviceIdType.MESH
BF = jnp.bfloat16
F32 = jnp.float32
I32 = jnp.int32
ROOT = 0.7071067811865476
ROOT_PI = 0.3989422804014327

T, D, F, CAP = 128, 1280, 640, 6
NZ, NX, NY = 8, 4, 4
Q, GS = 4, 8
RG = GS * CAP
M = 8 * RG
FW, BW = 1024, 512
PW = 3 * D + 128
CUT = 2048


def iota(shape, dim):
    return lax.broadcasted_iota(I32, shape, dim)


def onehot(cond):
    return jnp.where(cond, 1.0, 0.0).astype(BF)


def mm(a, b):
    return jnp.dot(a, b, preferred_element_type=F32)


def mm_nt(a, b):
    return lax.dot_general(a, b, (((1,), (1,)), ((), ())), preferred_element_type=F32)


def mm_tn(a, b):
    return lax.dot_general(a, b, (((0,), (0,)), ((), ())), preferred_element_type=F32)


def sixth(v):
    return ((v.astype(F32) + 0.5) * (1.0 / 6.0)).astype(I32)


def offset(k):
    pair = k // NX
    far = (pair + 1) // 2
    return far * (2 * (pair % 2) - 1), k % NX


def kernel(tok_ref, grad_ref, gate_ref, ids_ref, mod_ref, gain_ref, win_hbm, wout_hbm,
           gtok_ref, ggate_ref, gwin_hbm, gwout_hbm,
           out_buf, in_buf, rows, win, wout, pre, back, act16, pre16, part, sib, far, near, ret, home,
           acc_in, acc_out, st_in, st_out, tgt_s,
           w_sem, o_sem, as_sem, ar_sem, gs_sem, gr_sem, rs_sem, rr_sem, bs_sem, br_sem):
    dp, ex = lax.axis_index("dp"), lax.axis_index("expert")
    y, c = dp // 2, dp % 2
    z, x = ex // NX, ex % NX

    def column(step, core):
        return ((y + step + NY) % NY) * 2 + core

    up, down, other = {"dp": column(1, c)}, {"dp": column(-1, c)}, {"dp": y * 2 + 1 - c}

    def target(k):
        dz, dx = offset(k)
        return {"expert": ((z - dz + NZ) % NZ) * NX + (x - dx + NX) % NX}

    def source(k):
        dz, dx = offset(k)
        return {"expert": ((z + dz + NZ) % NZ) * NX + (x + dx) % NX}

    barrier = pltpu.get_barrier_semaphore()

    @pl.loop(1, NZ * NX)
    def _(k):
        pl.semaphore_signal(barrier, inc=1, device_id=target(k), device_id_type=MESH)

    for peer in (up, down, other):
        pl.semaphore_signal(barrier, inc=1, device_id=peer, device_id_type=MESH)

    load_in = pltpu.make_async_copy(win_hbm, win, w_sem.at[0])
    load_out = pltpu.make_async_copy(wout_hbm, wout, w_sem.at[1])
    load_in.start()
    load_out.start()

    def rdma(src, dst, ssem, rsem, dev):
        return pltpu.make_async_remote_copy(
            src_ref=src, dst_ref=dst, send_sem=ssem, recv_sem=rsem, device_id=dev, device_id_type=MESH
        )

    ids = ids_ref[...]
    wide = jnp.broadcast_to(ids.astype(F32), (T, T))
    same = (wide == wide.T) & (iota((T, T), 0) < iota((T, T), 1))
    slot = jnp.sum(jnp.where(same, 1.0, 0.0), axis=0, keepdims=True).astype(I32)
    tz, tx = ids >> 2, ids & 3
    dz = (z - tz + NZ) & (NZ - 1)
    pair = jnp.where(dz == 0, 0, jnp.where(dz <= NZ // 2, 2 * dz - 1, 2 * (NZ - dz)))
    first = (pair * NX + ((x - tx + NX) & (NX - 1))) * 16

    gate_col = jnp.broadcast_to(gate_ref[...].astype(F32), (T, T)).T[:, 0:1]
    mod_col = jnp.broadcast_to(mod_ref[...].astype(F32), (T, T)).T[:, 0:1]
    gain = jnp.where(mod_col == 1.0, gain_ref[1:2, :], gain_ref[0:1, :])
    tok = tok_ref[...]
    gated = (gate_col * gain * grad_ref[...].astype(F32)).astype(BF)

    def tail(piece, j):
        return jnp.where((piece & 3) == j, first + 12 + (piece >> 2), -1)

    where_rows = [first + slot, first + 6 + slot]
    where_tail = [[tail(slot, j), tail(slot + 6, j)] for j in range(4)]

    def pack(q):
        lines = iota((GS * 16, T), 0) + q * GS * 16
        body = [onehot(lines == w) for w in where_rows]
        for j in range(4):
            lhs = jnp.concatenate(body + [onehot(lines == w) for w in where_tail[j]], axis=1)
            cols = slice(256 * j, 256 * j + 256)
            rhs = jnp.concatenate([tok[:, cols], gated[:, cols], tok[:, FW:], gated[:, FW:]], axis=0)
            out_buf[q * GS:(q + 1) * GS, :, cols] = mm(lhs, rhs).astype(BF).reshape(GS, 16, 256)

    def a2a(k):
        return rdma(out_buf.at[k], in_buf.at[k], as_sem.at[k], ar_sem.at[k], target(k))

    for q in range(Q):
        pack(q)
        if q == 0:
            in_buf[0] = out_buf[0]
            pl.semaphore_wait(barrier, NZ * NX - 1 + 3)

        @pl.loop(max(1, q * GS), (q + 1) * GS)
        def _(k):
            a2a(k).start()

    cc = iota((1, GS * 16), 1)
    cs, ci = cc >> 4, cc & 15
    row_body = jnp.where(ci < 6, cs * 6 + ci, jnp.where(ci < 12, RG + cs * 6 + ci - 6, -1))

    def row_tail(j):
        p = (ci - 12) * 4 + j
        return jnp.where((ci >= 12) & (ci < 15), jnp.where(p < 6, cs * 6 + p, RG + cs * 6 + p - 6), -1)

    lines96 = iota((2 * RG, GS * 16), 0)
    un_body = onehot(lines96 == row_body)
    un_tail = jnp.concatenate([onehot(lines96 == row_tail(j)) for j in range(4)], axis=1)

    def gather(q, role):
        mine, below, above = dp, column(-1, c), column(1, c)
        beyond = column(2, c)
        d, half, dev = [
            (mine, None, up), (mine, None, down), (below, 0, up), (above, 1, down),
            (mine, None, other), (below, None, other), (above, None, other), (beyond, 0, other), (beyond, 1, other),
        ][role]
        ref = rows.at[q, d] if half is None else rows.at[q, d, half]
        return rdma(ref, ref, gs_sem.at[q, role], gr_sem.at[q, role], dev)

    def gather_wait(q, role):
        half = {2: 0, 3: 1, 7: 0, 8: 1}.get(role)
        d = {0: column(-1, c), 1: column(1, c), 2: column(2, c), 3: column(2, c), 4: column(0, 1 - c),
             5: column(-1, 1 - c), 6: column(1, 1 - c), 7: column(2, 1 - c), 8: column(2, 1 - c)}[role]
        ref = rows.at[q, d] if half is None else rows.at[q, d, half]
        rdma(ref, ref, gs_sem.at[q, role], gr_sem.at[q, role], other).wait_recv()

    def first_step(q):
        @pl.loop(max(1, q * GS), (q + 1) * GS)
        def _(k):
            a2a(k).wait_recv()

        got = in_buf[q * GS:(q + 1) * GS].reshape(GS * 16, FW)
        main = mm(un_body, got).astype(BF)
        stack = jnp.concatenate([got[:, 256 * j:256 * j + 256] for j in range(4)], axis=0)
        rest = mm(un_tail, stack).astype(BF)
        for h in range(2):
            rows[q, dp, h, :, 0:FW] = main[h * RG:(h + 1) * RG]
            rows[q, dp, h, :, FW:D] = rest[h * RG:(h + 1) * RG]
        for role in (0, 1, 4):
            gather(q, role).start()

    def second_step(q):
        gather_wait(q, 0)
        gather(q, 2).start()
        gather(q, 5).start()
        gather_wait(q, 1)
        gather(q, 3).start()
        gather(q, 6).start()

    def third_step(q):
        gather_wait(q, 2)
        gather(q, 7).start()
        gather_wait(q, 3)
        gather(q, 8).start()

    lane6 = iota((M, 128), 1)
    row_m = iota((M, 128), 0)
    gate_spread = lane6 == row_m - 6 * sixth(row_m)
    rr = iota((T, M), 0)
    gate_pick = onehot(((rr & 15) < 8) & (sixth(iota((T, M), 1)) == (rr >> 4) * 8 + (rr & 15)))

    def compute(q):
        for role in range(4, 9):
            gather_wait(q, role)
        pre[...] = mm(rows[q, :, 0].reshape(M, D), win[...])
        back[...] = mm_nt(rows[q, :, 1].reshape(M, D), wout[...])
        gates = []
        for r in range(0, M, 128):
            u = pre[r:r + 128]
            b = back[r:r + 128]
            cdf = 0.5 * (1.0 + lax.erf(u * ROOT))
            density = jnp.exp(-0.5 * u * u) * ROOT_PI
            act = u * cdf
            act16[q, r:r + 128] = act.astype(BF)
            pre16[q, r:r + 128] = (b * (cdf + u * density)).astype(BF)
            gates.append(jnp.sum(act * b, axis=1, keepdims=True))
        gate_sum = jnp.concatenate(gates, axis=0)
        spread = jnp.where(gate_spread, gate_sum, 0.0).astype(BF)
        part[q, :, :, 3 * D:PW] = mm(gate_pick, spread).astype(BF).reshape(8, 16, 128)
        tokens = mm_nt(pre16[q], win[...]).astype(BF).reshape(8, 3, 16, D)
        for g in range(3):
            part[q, :, :, g * D:(g + 1) * D] = tokens[:, g]
        for j in range(NY):
            pair_sum(q, j).start()

    def pair_sum(q, j):
        return rdma(part.at[q, column(j, 1 - c)], sib.at[q, j], rs_sem.at[q, j], rr_sem.at[q, j], other)

    def ring(q, role):
        src, dst, dev = [
            (part.at[q, column(2, c), :, 0:CUT], far.at[q, 0, :, 0:CUT], up),
            (part.at[q, column(2, c), :, CUT:PW], far.at[q, 1, :, 0:PW - CUT], down),
            (part.at[q, column(1, c)], near.at[q, 0], up),
            (part.at[q, column(-1, c)], near.at[q, 1], down),
        ][role]
        return rdma(src, dst, rs_sem.at[q, 4 + role], rr_sem.at[q, 4 + role], dev)

    def add_pair(q, j):
        pair_sum(q, j).wait_recv()
        d = column(j, c)
        part[q, d] = (part[q, d].astype(F32) + sib[q, j].astype(F32)).astype(BF)

    def reduce_far(q):
        add_pair(q, 2)
        ring(q, 0).start()
        ring(q, 1).start()

    def reduce_near(q):
        add_pair(q, 1)
        ring(q, 0).wait_recv()
        d = column(1, c)
        part[q, d, :, 0:CUT] = (part[q, d, :, 0:CUT].astype(F32) + far[q, 0].astype(F32)).astype(BF)
        ring(q, 2).start()
        add_pair(q, 3)
        ring(q, 1).wait_recv()
        d = column(-1, c)
        part[q, d, :, CUT:PW] = (part[q, d, :, CUT:PW].astype(F32) + far[q, 1, :, 0:PW - CUT].astype(F32)).astype(BF)
        ring(q, 3).start()

    br = iota((GS * 16, 3 * RG), 0)
    bs, bi = br >> 4, br & 15
    bc = iota((GS * 16, 3 * RG), 1)

    def back_pick(h):
        return onehot(bc == jnp.where(bi < 6, bs * 6 + bi, jnp.where(
            bi < 12, RG + bs * 6 + bi - 6, jnp.where(bi < 15, 2 * RG + bs * 6 + bi - 12 + 3 * h, -1))))

    back_picks = [back_pick(0), back_pick(1)]
    gr = iota((GS * 16, 16), 0)
    gate_line = onehot(((gr & 15) == 15) & (iota((GS * 16, 16), 1) == (gr >> 4)))

    def give_back(k):
        return rdma(ret.at[k], home.at[k], bs_sem.at[k], br_sem.at[k], source(k))

    def reduce_own(q):
        pair_sum(q, 0).wait_recv()
        total = part[q, dp].astype(F32) + sib[q, 0].astype(F32)
        ring(q, 2).wait_recv()
        ring(q, 3).wait_recv()
        total = (total + near[q, 0].astype(F32) + near[q, 1].astype(F32)).astype(BF)
        flat = jnp.concatenate([total[:, g * D:(g + 1) * D] for g in range(3)], axis=0)
        gates = mm(gate_line, total[:, 3 * D:PW])
        for h in range(2):
            rhs = jnp.concatenate(
                [flat[:, 256 * h:256 * h + 256], flat[:, 512 + 256 * h:768 + 256 * h], flat[:, 1024:1280]], axis=0
            )
            res = mm(back_picks[h], rhs)
            if h == 0:
                res = jnp.concatenate([res[:, 0:128] + gates, res[:, 128:256]], axis=1)
            ret[q * GS:(q + 1) * GS, :, 256 * h:256 * h + 256] = res.astype(BF).reshape(GS, 16, 256)
        if q == 0:
            home[0] = ret[0]

        @pl.loop(max(1, q * GS), (q + 1) * GS)
        def _(k):
            give_back(k).start()

    def weight_grads(half):
        q0 = 2 * half
        a = act16[q0:q0 + 2].reshape(2 * M, F)
        p = pre16[q0:q0 + 2].reshape(2 * M, F)
        g_all = rows[q0:q0 + 2, :, 1].reshape(2 * M, D)
        x_all = rows[q0:q0 + 2, :, 0].reshape(2 * M, D)
        go = mm_tn(a, g_all)
        gi = mm_tn(x_all, p)
        if half == 0:
            acc_out[...] = go
            acc_in[...] = gi
        else:
            st_out[...] = (acc_out[...] + go).astype(BF)
            st_in[...] = (acc_in[...] + gi).astype(BF)

    first_step(0)
    second_step(0)
    first_step(1)
    third_step(0)
    load_in.wait()
    load_out.wait()
    second_step(1)
    compute(0)
    first_step(2)
    third_step(1)
    reduce_far(0)
    second_step(2)
    reduce_near(0)
    compute(1)
    first_step(3)
    third_step(2)
    reduce_far(1)
    reduce_own(0)
    second_step(3)
    reduce_near(1)
    compute(2)
    third_step(3)
    reduce_far(2)
    reduce_own(1)
    weight_grads(0)
    reduce_near(2)
    compute(3)
    reduce_far(3)
    reduce_own(2)
    reduce_near(3)
    weight_grads(1)
    store_in = pltpu.make_async_copy(st_in, gwin_hbm, o_sem.at[0])
    store_out = pltpu.make_async_copy(st_out, gwout_hbm, o_sem.at[1])
    store_in.start()
    store_out.start()
    reduce_own(3)

    @pl.loop(1, NZ * NX)
    def _(k):
        give_back(k).wait_recv()

    tgt_s[...] = jnp.broadcast_to(first.astype(F32), (T, T)).T
    first_col = tgt_s[:, 0:1].astype(I32)
    slot_col = jnp.broadcast_to(slot.astype(F32), (T, T)).T[:, 0:1].astype(I32)
    lanes = iota((T, NZ * NX * 16), 1)
    back_rows = home[...].reshape(NZ * NX * 16, BW)
    gtok_ref[:, 0:512] = mm(onehot(lanes == first_col + slot_col), back_rows).astype(BF)
    gtok_ref[:, 512:1024] = mm(onehot(lanes == first_col + 6 + slot_col), back_rows).astype(BF)
    low = jnp.where(slot_col < 3, first_col + 12 + slot_col, -1)
    high = jnp.where(slot_col < 3, -1, first_col + 9 + slot_col)
    gtok_ref[:, 1024:1280] = (
        mm(onehot(lanes == low), back_rows[:, 0:256]) + mm(onehot(lanes == high), back_rows[:, 256:512])
    ).astype(BF)
    gate_lines = mm(onehot(lanes == first_col + 15), back_rows[:, 0:128])
    gate_tok = jnp.sum(jnp.where(iota((T, 128), 1) == slot_col, gate_lines, 0.0), axis=1, keepdims=True) / gate_col
    ggate_ref[...] = jnp.broadcast_to(gate_tok, (T, T)).T[0:1, :].astype(BF)

    @pl.loop(1, NZ * NX)
    def _(k):
        a2a(k).wait_send()
        give_back(k).wait_send()

    for q in range(Q):
        for role in range(9):
            gather(q, role).wait_send()
        for j in range(NY):
            pair_sum(q, j).wait_send()
        for role in range(4):
            ring(q, role).wait_send()
    store_in.wait()
    store_out.wait()


def local(tokens, grad_out, gate, expert_ids, modality, modal_gain, w_in, w_out):
    vmem = pl.BlockSpec(memory_space=pltpu.VMEM)
    hbm = pl.BlockSpec(memory_space=pl.ANY)
    dma = pltpu.SemaphoreType.DMA
    grad_tokens, grad_gate, grad_in, grad_out_w = pl.pallas_call(
        kernel,
        out_shape=[
            jax.ShapeDtypeStruct((T, D), BF),
            jax.ShapeDtypeStruct((1, T), BF),
            jax.ShapeDtypeStruct((D, F), BF),
            jax.ShapeDtypeStruct((F, D), BF),
        ],
        in_specs=[vmem] * 6 + [hbm] * 2,
        out_specs=[vmem, vmem, hbm, hbm],
        scratch_shapes=[
            pltpu.VMEM((NZ * NX, 16, FW), BF),
            pltpu.VMEM((NZ * NX, 16, FW), BF),
            pltpu.VMEM((Q, 8, 2, RG, D), BF),
            pltpu.VMEM((D, F), BF),
            pltpu.VMEM((F, D), BF),
            pltpu.VMEM((M, F), F32),
            pltpu.VMEM((M, F), F32),
            pltpu.VMEM((Q, M, F), BF),
            pltpu.VMEM((Q, M, F), BF),
            pltpu.VMEM((Q, 8, 16, PW), BF),
            pltpu.VMEM((Q, NY, 16, PW), BF),
            pltpu.VMEM((Q, 2, 16, CUT), BF),
            pltpu.VMEM((Q, 2, 16, PW), BF),
            pltpu.VMEM((NZ * NX, 16, BW), BF),
            pltpu.VMEM((NZ * NX, 16, BW), BF),
            pltpu.VMEM((D, F), F32),
            pltpu.VMEM((F, D), F32),
            pltpu.VMEM((D, F), BF),
            pltpu.VMEM((F, D), BF),
            pltpu.VMEM((T, T), F32),
            dma((2,)),
            dma((2,)),
            dma((NZ * NX,)),
            dma((NZ * NX,)),
            dma((Q, 9)),
            dma((Q, 9)),
            dma((Q, 8)),
            dma((Q, 8)),
            dma((NZ * NX,)),
            dma((NZ * NX,)),
        ],
        compiler_params=pltpu.CompilerParams(
            collective_id=0, has_side_effects=True, vmem_limit_bytes=56 * 1024 * 1024
        ),
        cost_estimate=pl.CostEstimate(flops=12_600_000_000, bytes_accessed=8_000_000, transcendentals=2_000_000),
    )(
        tokens,
        grad_out,
        gate.reshape(1, T),
        expert_ids.reshape(1, T),
        modality.reshape(1, T),
        modal_gain,
        w_in[0],
        w_out[0],
    )
    return grad_tokens, grad_gate.reshape(T), grad_in[None], grad_out_w[None]


def solution(mesh):
    rows = P(("dp", "expert"), None)
    flat = P(("dp", "expert"))
    return jax.shard_map(
        local,
        mesh=mesh,
        in_specs=(rows, rows, flat, rows, flat, P(), P("expert", None, "dp"), P("expert", "dp", None)),
        out_specs=(rows, flat, P("expert", None, "dp"), P("expert", "dp", None)),
        check_vma=False,
    )
```

```python
import functools

import jax
import jax.numpy as jnp
from jax import lax
from jax.experimental import pallas as pl
from jax.experimental.pallas import tpu as pltpu
from jax.sharding import PartitionSpec as P

MESH = pl.DeviceIdType.MESH
BF = jnp.bfloat16
F32 = jnp.float32
I32 = jnp.int32
ROOT = 0.7071067811865476
ROOT_PI = 0.3989422804014327

T, D, F, CAP = 128, 1280, 640, 6
NZ, NX, NY = 8, 4, 4
Q, GS = 4, 8
RG = GS * CAP
M = 8 * RG
FW, BW = 1024, 512
PW = 3 * D + 128
CUT = 2048


def iota(shape, dim):
    return lax.broadcasted_iota(I32, shape, dim)


def onehot(cond):
    return jnp.where(cond, 1.0, 0.0).astype(BF)


def mm(a, b):
    return jnp.dot(a, b, preferred_element_type=F32)


def mm_nt(a, b):
    return lax.dot_general(a, b, (((1,), (1,)), ((), ())), preferred_element_type=F32)


def mm_tn(a, b):
    return lax.dot_general(a, b, (((0,), (0,)), ((), ())), preferred_element_type=F32)


def sixth(v):
    return ((v.astype(F32) + 0.5) * (1.0 / 6.0)).astype(I32)


def offset(k):
    pair = k // NX
    far = (pair + 1) // 2
    return far * (2 * (pair % 2) - 1), k % NX


def as_column(row):
    return jnp.broadcast_to(row.astype(F32), (T, T)).T[:, 0:1]


def places(ids, z, x):
    wide = jnp.broadcast_to(ids.astype(F32), (T, T))
    same = (wide == wide.T) & (iota((T, T), 0) < iota((T, T), 1))
    slot = jnp.sum(jnp.where(same, 1.0, 0.0), axis=0, keepdims=True).astype(I32)
    dz = (z - (ids >> 2) + NZ) & (NZ - 1)
    pair = jnp.where(dz == 0, 0, jnp.where(dz <= NZ // 2, 2 * dz - 1, 2 * (NZ - dz)))
    return (pair * NX + ((x - (ids & 3) + NX) & (NX - 1))) * 16, slot


def kernel(tok_ref, grad_ref, gate_ref, ids_ref, mod_ref, gain_ref, win_hbm, wout_hbm,
           home, gwin_hbm, gwout_hbm,
           out_buf, in_buf, rows, win, wout, pre, back, act16, pre16, part, sib, far, near, ret,
           acc_in, acc_out, st_in, st_out,
           w_sem, o_sem, as_sem, ar_sem, gs_sem, gr_sem, rs_sem, rr_sem, bs_sem, br_sem):
    dp, ex = lax.axis_index("dp"), lax.axis_index("expert")
    y, c = dp // 2, dp % 2
    z, x = ex // NX, ex % NX

    def column(step, core):
        return ((y + step + NY) % NY) * 2 + core

    up, down, other = {"dp": column(1, c)}, {"dp": column(-1, c)}, {"dp": y * 2 + 1 - c}

    def target(k):
        dz, dx = offset(k)
        return {"expert": ((z - dz + NZ) % NZ) * NX + (x - dx + NX) % NX}

    def source(k):
        dz, dx = offset(k)
        return {"expert": ((z + dz + NZ) % NZ) * NX + (x + dx) % NX}

    barrier = pltpu.get_barrier_semaphore()

    @pl.loop(1, NZ * NX)
    def _(k):
        pl.semaphore_signal(barrier, inc=1, device_id=target(k), device_id_type=MESH)

    for peer in (up, down, other):
        pl.semaphore_signal(barrier, inc=1, device_id=peer, device_id_type=MESH)

    load_in = pltpu.make_async_copy(win_hbm, win, w_sem.at[0])
    load_out = pltpu.make_async_copy(wout_hbm, wout, w_sem.at[1])
    load_in.start()
    load_out.start()

    def rdma(src, dst, ssem, rsem, dev):
        return pltpu.make_async_remote_copy(
            src_ref=src, dst_ref=dst, send_sem=ssem, recv_sem=rsem, device_id=dev, device_id_type=MESH
        )

    first, slot = places(ids_ref[...], z, x)
    gate_col = as_column(gate_ref[...])
    mod_col = as_column(mod_ref[...])
    gain = jnp.where(mod_col == 1.0, gain_ref[1:2, :], gain_ref[0:1, :])
    tok = tok_ref[...]
    gated = (gate_col * gain * grad_ref[...].astype(F32)).astype(BF)

    def tail(piece, j):
        return jnp.where((piece & 3) == j, first + 12 + (piece >> 2), -1)

    where_rows = [first + slot, first + 6 + slot]
    where_tail = [[tail(slot, j), tail(slot + 6, j)] for j in range(4)]

    def pack(q):
        lines = iota((GS * 16, T), 0) + q * GS * 16
        body = [onehot(lines == w) for w in where_rows]
        for j in range(4):
            lhs = jnp.concatenate(body + [onehot(lines == w) for w in where_tail[j]], axis=1)
            cols = slice(256 * j, 256 * j + 256)
            rhs = jnp.concatenate([tok[:, cols], gated[:, cols], tok[:, FW:], gated[:, FW:]], axis=0)
            out_buf[q * GS:(q + 1) * GS, :, cols] = mm(lhs, rhs).astype(BF).reshape(GS, 16, 256)

    def a2a(k):
        return rdma(out_buf.at[k], in_buf.at[k], as_sem.at[k], ar_sem.at[k], target(k))

    def dispatch(q):
        @pl.loop(max(1, q * GS), (q + 1) * GS)
        def _(k):
            a2a(k).start()

    for q in range(Q):
        pack(q)
        if q == 0:
            in_buf[0] = out_buf[0]
            pl.semaphore_wait(barrier, NZ * NX - 1 + 3)
        if q < 2:
            dispatch(q)

    cc = iota((1, GS * 16), 1)
    cs, ci = cc >> 4, cc & 15
    row_body = jnp.where(ci < 6, cs * 6 + ci, jnp.where(ci < 12, RG + cs * 6 + ci - 6, -1))

    def row_tail(j):
        p = (ci - 12) * 4 + j
        return jnp.where((ci >= 12) & (ci < 15), jnp.where(p < 6, cs * 6 + p, RG + cs * 6 + p - 6), -1)

    lines96 = iota((2 * RG, GS * 16), 0)
    un_body = onehot(lines96 == row_body)
    un_tail = jnp.concatenate([onehot(lines96 == row_tail(j)) for j in range(4)], axis=1)

    def gather(q, role):
        mine, below, above = dp, column(-1, c), column(1, c)
        beyond = column(2, c)
        d, half, dev = [
            (mine, None, up), (mine, None, down), (below, 0, up), (above, 1, down),
            (mine, None, other), (below, None, other), (above, None, other), (beyond, 0, other), (beyond, 1, other),
        ][role]
        ref = rows.at[q, d] if half is None else rows.at[q, d, half]
        return rdma(ref, ref, gs_sem.at[q, role], gr_sem.at[q, role], dev)

    def gather_wait(q, role):
        half = {2: 0, 3: 1, 7: 0, 8: 1}.get(role)
        d = {0: column(-1, c), 1: column(1, c), 2: column(2, c), 3: column(2, c), 4: column(0, 1 - c),
             5: column(-1, 1 - c), 6: column(1, 1 - c), 7: column(2, 1 - c), 8: column(2, 1 - c)}[role]
        ref = rows.at[q, d] if half is None else rows.at[q, d, half]
        rdma(ref, ref, gs_sem.at[q, role], gr_sem.at[q, role], other).wait_recv()

    def first_step(q):
        @pl.loop(max(1, q * GS), (q + 1) * GS)
        def _(k):
            a2a(k).wait_recv()

        got = in_buf[q * GS:(q + 1) * GS].reshape(GS * 16, FW)
        main = mm(un_body, got).astype(BF)
        stack = jnp.concatenate([got[:, 256 * j:256 * j + 256] for j in range(4)], axis=0)
        rest = mm(un_tail, stack).astype(BF)
        for h in range(2):
            rows[q, dp, h, :, 0:FW] = main[h * RG:(h + 1) * RG]
            rows[q, dp, h, :, FW:D] = rest[h * RG:(h + 1) * RG]
        for role in (0, 1, 4):
            gather(q, role).start()
        if q < 2:
            dispatch(q + 2)

    def second_step(q):
        gather_wait(q, 0)
        gather(q, 2).start()
        gather(q, 5).start()
        gather_wait(q, 1)
        gather(q, 3).start()
        gather(q, 6).start()

    def third_step(q):
        gather_wait(q, 2)
        gather(q, 7).start()
        gather_wait(q, 3)
        gather(q, 8).start()

    lane6 = iota((M, 128), 1)
    row_m = iota((M, 128), 0)
    gate_spread = lane6 == row_m - 6 * sixth(row_m)
    rr = iota((T, M), 0)
    gate_pick = onehot(((rr & 15) < 8) & (sixth(iota((T, M), 1)) == (rr >> 4) * 8 + (rr & 15)))

    def compute(q):
        for role in range(4, 9):
            gather_wait(q, role)
        if q == 0:
            load_in.wait()
            load_out.wait()
        pre[...] = mm(rows[q, :, 0].reshape(M, D), win[...])
        back[...] = mm_nt(rows[q, :, 1].reshape(M, D), wout[...])
        gates = []
        for r in range(0, M, 128):
            u = pre[r:r + 128]
            b = back[r:r + 128]
            cdf = 0.5 * (1.0 + lax.erf(u * ROOT))
            density = jnp.exp(-0.5 * u * u) * ROOT_PI
            act = u * cdf
            act16[q, r:r + 128] = act.astype(BF)
            pre16[q, r:r + 128] = (b * (cdf + u * density)).astype(BF)
            gates.append(jnp.sum(act * b, axis=1, keepdims=True))
        gate_sum = jnp.concatenate(gates, axis=0)
        spread = jnp.where(gate_spread, gate_sum, 0.0).astype(BF)
        part[q, :, :, 3 * D:PW] = mm(gate_pick, spread).astype(BF).reshape(8, 16, 128)
        tokens = mm_nt(pre16[q], win[...]).astype(BF).reshape(8, 3, 16, D)
        for g in range(3):
            part[q, :, :, g * D:(g + 1) * D] = tokens[:, g]
        for j in range(NY):
            pair_sum(q, j).start()

    def pair_sum(q, j):
        return rdma(part.at[q, column(j, 1 - c)], sib.at[q, j], rs_sem.at[q, j], rr_sem.at[q, j], other)

    def ring(q, role):
        src, dst, dev = [
            (part.at[q, column(2, c), :, 0:CUT], far.at[q, 0, :, 0:CUT], up),
            (part.at[q, column(2, c), :, CUT:PW], far.at[q, 1, :, 0:PW - CUT], down),
            (part.at[q, column(1, c)], near.at[q, 0], up),
            (part.at[q, column(-1, c)], near.at[q, 1], down),
        ][role]
        return rdma(src, dst, rs_sem.at[q, 4 + role], rr_sem.at[q, 4 + role], dev)

    def add_pair(q, j):
        pair_sum(q, j).wait_recv()
        d = column(j, c)
        part[q, d] = (part[q, d].astype(F32) + sib[q, j].astype(F32)).astype(BF)

    def reduce_far(q):
        add_pair(q, 2)
        ring(q, 0).start()
        ring(q, 1).start()

    def reduce_near(q):
        add_pair(q, 1)
        ring(q, 0).wait_recv()
        d = column(1, c)
        part[q, d, :, 0:CUT] = (part[q, d, :, 0:CUT].astype(F32) + far[q, 0].astype(F32)).astype(BF)
        ring(q, 2).start()
        add_pair(q, 3)
        ring(q, 1).wait_recv()
        d = column(-1, c)
        part[q, d, :, CUT:PW] = (part[q, d, :, CUT:PW].astype(F32) + far[q, 1, :, 0:PW - CUT].astype(F32)).astype(BF)
        ring(q, 3).start()

    br = iota((GS * 16, 3 * RG), 0)
    bs, bi = br >> 4, br & 15
    bc = iota((GS * 16, 3 * RG), 1)

    def back_pick(h):
        return onehot(bc == jnp.where(bi < 6, bs * 6 + bi, jnp.where(
            bi < 12, RG + bs * 6 + bi - 6, jnp.where(bi < 15, 2 * RG + bs * 6 + bi - 12 + 3 * h, -1))))

    back_picks = [back_pick(0), back_pick(1)]
    gr = iota((GS * 16, 16), 0)
    gate_line = onehot(((gr & 15) == 15) & (iota((GS * 16, 16), 1) == (gr >> 4)))

    def give_back(k):
        return rdma(ret.at[k], home.at[k], bs_sem.at[k], br_sem.at[k], source(k))

    keep = pltpu.make_async_copy(ret.at[0], home.at[0], w_sem.at[2])

    def reduce_own(q):
        pair_sum(q, 0).wait_recv()
        total = part[q, dp].astype(F32) + sib[q, 0].astype(F32)
        ring(q, 2).wait_recv()
        ring(q, 3).wait_recv()
        total = (total + near[q, 0].astype(F32) + near[q, 1].astype(F32)).astype(BF)
        flat = jnp.concatenate([total[:, g * D:(g + 1) * D] for g in range(3)], axis=0)
        gates = mm(gate_line, total[:, 3 * D:PW])
        for h in range(2):
            rhs = jnp.concatenate(
                [flat[:, 256 * h:256 * h + 256], flat[:, 512 + 256 * h:768 + 256 * h], flat[:, 1024:1280]], axis=0
            )
            res = mm(back_picks[h], rhs)
            if h == 0:
                res = jnp.concatenate([res[:, 0:128] + gates, res[:, 128:256]], axis=1)
            ret[q * GS:(q + 1) * GS, :, 256 * h:256 * h + 256] = res.astype(BF).reshape(GS, 16, 256)
        if q == 0:
            keep.start()

        @pl.loop(max(1, q * GS), (q + 1) * GS)
        def _(k):
            give_back(k).start()

    def weight_grads(half):
        q0 = 2 * half
        a = act16[q0:q0 + 2].reshape(2 * M, F)
        p = pre16[q0:q0 + 2].reshape(2 * M, F)
        g_all = rows[q0:q0 + 2, :, 1].reshape(2 * M, D)
        x_all = rows[q0:q0 + 2, :, 0].reshape(2 * M, D)
        go = mm_tn(a, g_all)
        gi = mm_tn(x_all, p)
        if half == 0:
            acc_out[...] = go
            acc_in[...] = gi
        else:
            st_out[...] = (acc_out[...] + go).astype(BF)
            st_in[...] = (acc_in[...] + gi).astype(BF)

    first_step(0)
    first_step(1)
    second_step(0)
    first_step(2)
    third_step(0)
    second_step(1)
    compute(0)
    first_step(3)
    third_step(1)
    second_step(2)
    reduce_far(0)
    compute(1)
    third_step(2)
    second_step(3)
    reduce_near(0)
    reduce_far(1)
    compute(2)
    third_step(3)
    reduce_near(1)
    reduce_far(2)
    reduce_own(0)
    weight_grads(0)
    compute(3)
    reduce_near(2)
    reduce_own(1)
    reduce_far(3)
    reduce_own(2)
    reduce_near(3)
    weight_grads(1)
    reduce_own(3)
    store_in = pltpu.make_async_copy(st_in, gwin_hbm, o_sem.at[0])
    store_out = pltpu.make_async_copy(st_out, gwout_hbm, o_sem.at[1])
    store_in.start()
    store_out.start()

    @pl.loop(1, NZ * NX)
    def _(k):
        give_back(k).wait_recv()

    @pl.loop(1, NZ * NX)
    def _(k):
        a2a(k).wait_send()
        give_back(k).wait_send()

    for q in range(Q):
        for role in range(9):
            gather(q, role).wait_send()
        for j in range(NY):
            pair_sum(q, j).wait_send()
        for role in range(4):
            ring(q, role).wait_send()
    keep.wait()
    store_in.wait()
    store_out.wait()


def finish(ids_ref, gate_ref, home_hbm, gwin_in, gwout_in, gtok_ref, ggate_ref, gwin_hbm, gwout_hbm, home, sem):
    copies = [
        pltpu.make_async_copy(home_hbm, home, sem.at[0]),
        pltpu.make_async_copy(gwin_in, gwin_hbm, sem.at[1]),
        pltpu.make_async_copy(gwout_in, gwout_hbm, sem.at[2]),
    ]
    for copy in copies:
        copy.start()
    ex = lax.axis_index("expert")
    first, slot = places(ids_ref[...], ex // NX, ex % NX)
    first, slot = as_column(first).astype(I32), as_column(slot).astype(I32)
    gate = as_column(gate_ref[...])
    lanes = iota((T, NZ * NX * 16), 1)
    copies[0].wait()
    lines = home[...].reshape(NZ * NX * 16, BW)
    gtok_ref[:, 0:512] = mm(onehot(lanes == first + slot), lines).astype(BF)
    gtok_ref[:, 512:1024] = mm(onehot(lanes == first + 6 + slot), lines).astype(BF)
    low = jnp.where(slot < 3, first + 12 + slot, -1)
    high = jnp.where(slot < 3, -1, first + 9 + slot)
    gtok_ref[:, 1024:1280] = (
        mm(onehot(lanes == low), lines[:, 0:256]) + mm(onehot(lanes == high), lines[:, 256:512])
    ).astype(BF)
    gate_lines = mm(onehot(lanes == first + 15), lines[:, 0:128])
    gate_tok = jnp.sum(jnp.where(iota((T, 128), 1) == slot, gate_lines, 0.0), axis=1, keepdims=True) / gate
    ggate_ref[...] = jnp.broadcast_to(gate_tok, (T, T)).T[0:1, :].astype(BF)
    copies[1].wait()
    copies[2].wait()


def local(tokens, grad_out, gate, expert_ids, modality, modal_gain, w_in, w_out):
    vmem = pl.BlockSpec(memory_space=pltpu.VMEM)
    hbm = pl.BlockSpec(memory_space=pl.ANY)
    dma = pltpu.SemaphoreType.DMA
    gate_row, ids_row = gate.reshape(1, T), expert_ids.reshape(1, T)
    weights = [jax.ShapeDtypeStruct((D, F), BF), jax.ShapeDtypeStruct((F, D), BF)]
    home, in_part, out_part = pl.pallas_call(
        kernel,
        out_shape=[jax.ShapeDtypeStruct((NZ * NX, 16, BW), BF)] + weights,
        in_specs=[vmem] * 6 + [hbm] * 2,
        out_specs=[hbm] * 3,
        scratch_shapes=[
            pltpu.VMEM((NZ * NX, 16, FW), BF),
            pltpu.VMEM((NZ * NX, 16, FW), BF),
            pltpu.VMEM((Q, 8, 2, RG, D), BF),
            pltpu.VMEM((D, F), BF),
            pltpu.VMEM((F, D), BF),
            pltpu.VMEM((M, F), F32),
            pltpu.VMEM((M, F), F32),
            pltpu.VMEM((Q, M, F), BF),
            pltpu.VMEM((Q, M, F), BF),
            pltpu.VMEM((Q, 8, 16, PW), BF),
            pltpu.VMEM((Q, NY, 16, PW), BF),
            pltpu.VMEM((Q, 2, 16, CUT), BF),
            pltpu.VMEM((Q, 2, 16, PW), BF),
            pltpu.VMEM((NZ * NX, 16, BW), BF),
            pltpu.VMEM((D, F), F32),
            pltpu.VMEM((F, D), F32),
            pltpu.VMEM((D, F), BF),
            pltpu.VMEM((F, D), BF),
            dma((3,)),
            dma((2,)),
            dma((NZ * NX,)),
            dma((NZ * NX,)),
            dma((Q, 9)),
            dma((Q, 9)),
            dma((Q, 8)),
            dma((Q, 8)),
            dma((NZ * NX,)),
            dma((NZ * NX,)),
        ],
        compiler_params=pltpu.CompilerParams(
            collective_id=0, has_side_effects=True, vmem_limit_bytes=56 * 1024 * 1024
        ),
        cost_estimate=pl.CostEstimate(flops=12_600_000_000, bytes_accessed=8_000_000, transcendentals=2_000_000),
    )(
        tokens,
        grad_out,
        gate_row,
        ids_row,
        modality.reshape(1, T),
        modal_gain,
        w_in[0],
        w_out[0],
    )
    grad_tokens, grad_gate, grad_in, grad_out_w = pl.pallas_call(
        finish,
        out_shape=[jax.ShapeDtypeStruct((T, D), BF), jax.ShapeDtypeStruct((1, T), BF)] + weights,
        in_specs=[vmem] * 2 + [hbm] * 3,
        out_specs=[vmem] * 2 + [hbm] * 2,
        scratch_shapes=[pltpu.VMEM((NZ * NX, 16, BW), BF), dma((3,))],
        compiler_params=pltpu.CompilerParams(vmem_limit_bytes=16 * 1024 * 1024),
    )(ids_row, gate_row, home, in_part, out_part)
    return grad_tokens, grad_gate.reshape(T), grad_in[None], grad_out_w[None]


def solution(mesh):
    rows = P(("dp", "expert"), None)
    flat = P(("dp", "expert"))
    return jax.shard_map(
        local,
        mesh=mesh,
        in_specs=(rows, rows, flat, rows, flat, P(), P("expert", None, "dp"), P("expert", "dp", None)),
        out_specs=(rows, flat, P("expert", None, "dp"), P("expert", "dp", None)),
        check_vma=False,
    )
```

```python
import functools

import jax
import jax.numpy as jnp
from jax import lax
from jax.experimental import pallas as pl
from jax.experimental.pallas import tpu as pltpu
from jax.sharding import PartitionSpec as P

MESH = pl.DeviceIdType.MESH
BF = jnp.bfloat16
F32 = jnp.float32
I32 = jnp.int32
ROOT = 0.7071067811865476
ROOT_PI = 0.3989422804014327

T, D, F, CAP = 128, 1280, 640, 6
NZ, NX, NY = 8, 4, 4
Q, GS = 4, 8
RG = GS * CAP
M = 8 * RG
FW, BW = 1024, 512
PW = 3 * D + 128
CUT = 2048


def iota(shape, dim):
    return lax.broadcasted_iota(I32, shape, dim)


def onehot(cond):
    return jnp.where(cond, 1.0, 0.0).astype(BF)


def mm(a, b):
    return jnp.dot(a, b, preferred_element_type=F32)


def mm_nt(a, b):
    return lax.dot_general(a, b, (((1,), (1,)), ((), ())), preferred_element_type=F32)


def mm_tn(a, b):
    return lax.dot_general(a, b, (((0,), (0,)), ((), ())), preferred_element_type=F32)


def sixth(v):
    return ((v.astype(F32) + 0.5) * (1.0 / 6.0)).astype(I32)


def offset(k):
    pair = k // NX
    far = (pair + 1) // 2
    return far * (2 * (pair % 2) - 1), k % NX


def as_column(row):
    return jnp.broadcast_to(row.astype(F32), (T, T)).T[:, 0:1]


def places(ids, z, x):
    wide = jnp.broadcast_to(ids.astype(F32), (T, T))
    same = (wide == wide.T) & (iota((T, T), 0) < iota((T, T), 1))
    slot = jnp.sum(jnp.where(same, 1.0, 0.0), axis=0, keepdims=True).astype(I32)
    dz = (z - (ids >> 2) + NZ) & (NZ - 1)
    pair = jnp.where(dz == 0, 0, jnp.where(dz <= NZ // 2, 2 * dz - 1, 2 * (NZ - dz)))
    return (pair * NX + ((x - (ids & 3) + NX) & (NX - 1))) * 16, slot


def kernel(tok_ref, grad_ref, gate_ref, ids_ref, mod_ref, gain_ref, win_hbm, wout_hbm,
           home, gwin_hbm, gwout_hbm,
           out_buf, in_buf, rows, win, wout, pre, back, act16, pre16, part, sib, far, near, ret,
           acc_in, acc_out, st_in, st_out,
           w_sem, o_sem, as_sem, ar_sem, gs_sem, gr_sem, rs_sem, rr_sem, bs_sem, br_sem):
    dp, ex = lax.axis_index("dp"), lax.axis_index("expert")
    y, c = dp // 2, dp % 2
    z, x = ex // NX, ex % NX

    def column(step, core):
        return ((y + step + NY) % NY) * 2 + core

    up, down, other = {"dp": column(1, c)}, {"dp": column(-1, c)}, {"dp": y * 2 + 1 - c}

    def target(k):
        dz, dx = offset(k)
        return {"expert": ((z - dz + NZ) % NZ) * NX + (x - dx + NX) % NX}

    def source(k):
        dz, dx = offset(k)
        return {"expert": ((z + dz + NZ) % NZ) * NX + (x + dx) % NX}

    barrier = pltpu.get_barrier_semaphore()

    @pl.loop(1, NZ * NX)
    def _(k):
        pl.semaphore_signal(barrier, inc=1, device_id=target(k), device_id_type=MESH)

    for peer in (up, down, other):
        pl.semaphore_signal(barrier, inc=1, device_id=peer, device_id_type=MESH)

    load_in = pltpu.make_async_copy(win_hbm, win, w_sem.at[0])
    load_out = pltpu.make_async_copy(wout_hbm, wout, w_sem.at[1])
    load_in.start()
    load_out.start()

    def rdma(src, dst, ssem, rsem, dev):
        return pltpu.make_async_remote_copy(
            src_ref=src, dst_ref=dst, send_sem=ssem, recv_sem=rsem, device_id=dev, device_id_type=MESH
        )

    first, slot = places(ids_ref[...], z, x)
    gate_col = as_column(gate_ref[...])
    mod_col = as_column(mod_ref[...])
    gain = jnp.where(mod_col == 1.0, gain_ref[1:2, :], gain_ref[0:1, :])
    tok = tok_ref[...]
    gated = (gate_col * gain * grad_ref[...].astype(F32)).astype(BF)

    def tail(piece, j):
        return jnp.where((piece & 3) == j, first + 12 + (piece >> 2), -1)

    where_rows = [first + slot, first + 6 + slot]
    where_tail = [[tail(slot, j), tail(slot + 6, j)] for j in range(4)]

    def pack(q):
        lines = iota((GS * 16, T), 0) + q * GS * 16
        body = [onehot(lines == w) for w in where_rows]
        for j in range(4):
            lhs = jnp.concatenate(body + [onehot(lines == w) for w in where_tail[j]], axis=1)
            cols = slice(256 * j, 256 * j + 256)
            rhs = jnp.concatenate([tok[:, cols], gated[:, cols], tok[:, FW:], gated[:, FW:]], axis=0)
            out_buf[q * GS:(q + 1) * GS, :, cols] = mm(lhs, rhs).astype(BF).reshape(GS, 16, 256)

    def a2a(k):
        return rdma(out_buf.at[k], in_buf.at[k], as_sem.at[k], ar_sem.at[k], target(k))

    def dispatch(q):
        @pl.loop(max(1, q * GS), (q + 1) * GS)
        def _(k):
            a2a(k).start()

    for q in range(Q):
        pack(q)
        if q == 0:
            in_buf[0] = out_buf[0]
            pl.semaphore_wait(barrier, NZ * NX - 1 + 3)
        if q < 2:
            dispatch(q)

    cc = iota((1, GS * 16), 1)
    cs, ci = cc >> 4, cc & 15
    row_body = jnp.where(ci < 6, cs * 6 + ci, jnp.where(ci < 12, RG + cs * 6 + ci - 6, -1))

    def row_tail(j):
        p = (ci - 12) * 4 + j
        return jnp.where((ci >= 12) & (ci < 15), jnp.where(p < 6, cs * 6 + p, RG + cs * 6 + p - 6), -1)

    lines96 = iota((2 * RG, GS * 16), 0)
    un_body = onehot(lines96 == row_body)
    un_tail = jnp.concatenate([onehot(lines96 == row_tail(j)) for j in range(4)], axis=1)

    def gather(q, role):
        mine, below, above = dp, column(-1, c), column(1, c)
        beyond = column(2, c)
        d, half, dev = [
            (mine, None, up), (mine, None, down), (below, 0, up), (above, 1, down),
            (mine, None, other), (below, None, other), (above, None, other), (beyond, 0, other), (beyond, 1, other),
        ][role]
        ref = rows.at[q, d] if half is None else rows.at[q, d, half]
        return rdma(ref, ref, gs_sem.at[q, role], gr_sem.at[q, role], dev)

    def gather_wait(q, role):
        half = {2: 0, 3: 1, 7: 0, 8: 1}.get(role)
        d = {0: column(-1, c), 1: column(1, c), 2: column(2, c), 3: column(2, c), 4: column(0, 1 - c),
             5: column(-1, 1 - c), 6: column(1, 1 - c), 7: column(2, 1 - c), 8: column(2, 1 - c)}[role]
        ref = rows.at[q, d] if half is None else rows.at[q, d, half]
        rdma(ref, ref, gs_sem.at[q, role], gr_sem.at[q, role], other).wait_recv()

    def first_step(q):
        @pl.loop(max(1, q * GS), (q + 1) * GS)
        def _(k):
            a2a(k).wait_recv()

        got = in_buf[q * GS:(q + 1) * GS].reshape(GS * 16, FW)
        main = mm(un_body, got).astype(BF)
        stack = jnp.concatenate([got[:, 256 * j:256 * j + 256] for j in range(4)], axis=0)
        rest = mm(un_tail, stack).astype(BF)
        for h in range(2):
            rows[q, dp, h, :, 0:FW] = main[h * RG:(h + 1) * RG]
            rows[q, dp, h, :, FW:D] = rest[h * RG:(h + 1) * RG]
        for role in (0, 1, 4):
            gather(q, role).start()
        if q < 2:
            dispatch(q + 2)

    def second_step(q):
        gather_wait(q, 0)
        gather(q, 2).start()
        gather(q, 5).start()
        gather_wait(q, 1)
        gather(q, 3).start()
        gather(q, 6).start()

    def third_step(q):
        gather_wait(q, 2)
        gather(q, 7).start()
        gather_wait(q, 3)
        gather(q, 8).start()

    lane6 = iota((M, 128), 1)
    row_m = iota((M, 128), 0)
    gate_spread = lane6 == row_m - 6 * sixth(row_m)
    rr = iota((T, M), 0)
    gate_pick = onehot(((rr & 15) < 8) & (sixth(iota((T, M), 1)) == (rr >> 4) * 8 + (rr & 15)))

    def compute(q):
        for role in range(4, 9):
            gather_wait(q, role)
        if q == 0:
            load_in.wait()
            load_out.wait()
        pre[...] = mm(rows[q, :, 0].reshape(M, D), win[...])
        back[...] = mm_nt(rows[q, :, 1].reshape(M, D), wout[...])
        gates = []
        for r in range(0, M, 128):
            u = pre[r:r + 128]
            b = back[r:r + 128]
            cdf = 0.5 * (1.0 + lax.erf(u * ROOT))
            density = jnp.exp(-0.5 * u * u) * ROOT_PI
            act = u * cdf
            act16[q, r:r + 128] = act.astype(BF)
            pre16[q, r:r + 128] = (b * (cdf + u * density)).astype(BF)
            gates.append(jnp.sum(act * b, axis=1, keepdims=True))
        gate_sum = jnp.concatenate(gates, axis=0)
        spread = jnp.where(gate_spread, gate_sum, 0.0).astype(BF)
        part[q, :, :, 3 * D:PW] = mm(gate_pick, spread).astype(BF).reshape(8, 16, 128)
        tokens = mm_nt(pre16[q], win[...]).astype(BF).reshape(8, 3, 16, D)
        for g in range(3):
            part[q, :, :, g * D:(g + 1) * D] = tokens[:, g]
        for j in range(NY):
            pair_sum(q, j).start()

    def pair_sum(q, j):
        return rdma(part.at[q, column(j, 1 - c)], sib.at[q, j], rs_sem.at[q, j], rr_sem.at[q, j], other)

    def ring(q, role):
        src, dst, dev = [
            (part.at[q, column(2, c), :, 0:CUT], far.at[q, 0, :, 0:CUT], up),
            (part.at[q, column(2, c), :, CUT:PW], far.at[q, 1, :, 0:PW - CUT], down),
            (part.at[q, column(1, c)], near.at[q, 0], up),
            (part.at[q, column(-1, c)], near.at[q, 1], down),
        ][role]
        return rdma(src, dst, rs_sem.at[q, 4 + role], rr_sem.at[q, 4 + role], dev)

    def add_pair(q, j):
        pair_sum(q, j).wait_recv()
        d = column(j, c)
        part[q, d] = (part[q, d].astype(F32) + sib[q, j].astype(F32)).astype(BF)

    def reduce_far(q):
        add_pair(q, 2)
        ring(q, 0).start()
        ring(q, 1).start()

    def reduce_near(q):
        add_pair(q, 1)
        ring(q, 0).wait_recv()
        d = column(1, c)
        part[q, d, :, 0:CUT] = (part[q, d, :, 0:CUT].astype(F32) + far[q, 0].astype(F32)).astype(BF)
        ring(q, 2).start()
        add_pair(q, 3)
        ring(q, 1).wait_recv()
        d = column(-1, c)
        part[q, d, :, CUT:PW] = (part[q, d, :, CUT:PW].astype(F32) + far[q, 1, :, 0:PW - CUT].astype(F32)).astype(BF)
        ring(q, 3).start()

    br = iota((GS * 16, 3 * RG), 0)
    bs, bi = br >> 4, br & 15
    bc = iota((GS * 16, 3 * RG), 1)

    def back_pick(h):
        return onehot(bc == jnp.where(bi < 6, bs * 6 + bi, jnp.where(
            bi < 12, RG + bs * 6 + bi - 6, jnp.where(bi < 15, 2 * RG + bs * 6 + bi - 12 + 3 * h, -1))))

    back_picks = [back_pick(0), back_pick(1)]
    gr = iota((GS * 16, 16), 0)
    gate_line = onehot(((gr & 15) == 15) & (iota((GS * 16, 16), 1) == (gr >> 4)))

    def give_back(k):
        return rdma(ret.at[k], home.at[k], bs_sem.at[k], br_sem.at[k], source(k))

    keep = pltpu.make_async_copy(ret.at[0], home.at[0], w_sem.at[2])

    def reduce_own(q):
        pair_sum(q, 0).wait_recv()
        total = part[q, dp].astype(F32) + sib[q, 0].astype(F32)
        ring(q, 2).wait_recv()
        ring(q, 3).wait_recv()
        total = (total + near[q, 0].astype(F32) + near[q, 1].astype(F32)).astype(BF)
        flat = jnp.concatenate([total[:, g * D:(g + 1) * D] for g in range(3)], axis=0)
        gates = mm(gate_line, total[:, 3 * D:PW])
        for h in range(2):
            rhs = jnp.concatenate(
                [flat[:, 256 * h:256 * h + 256], flat[:, 512 + 256 * h:768 + 256 * h], flat[:, 1024:1280]], axis=0
            )
            res = mm(back_picks[h], rhs)
            if h == 0:
                res = jnp.concatenate([res[:, 0:128] + gates, res[:, 128:256]], axis=1)
            ret[q * GS:(q + 1) * GS, :, 256 * h:256 * h + 256] = res.astype(BF).reshape(GS, 16, 256)
        if q == 0:
            keep.start()

        @pl.loop(max(1, q * GS), (q + 1) * GS)
        def _(k):
            give_back(k).start()

    def weight_grads(half):
        q0 = 2 * half
        a = act16[q0:q0 + 2].reshape(2 * M, F)
        p = pre16[q0:q0 + 2].reshape(2 * M, F)
        g_all = rows[q0:q0 + 2, :, 1].reshape(2 * M, D)
        x_all = rows[q0:q0 + 2, :, 0].reshape(2 * M, D)
        go = mm_tn(a, g_all)
        gi = mm_tn(x_all, p)
        if half == 0:
            acc_out[...] = go
            acc_in[...] = gi
        else:
            st_out[...] = (acc_out[...] + go).astype(BF)
            st_in[...] = (acc_in[...] + gi).astype(BF)

    first_step(0)
    first_step(1)
    second_step(0)
    first_step(2)
    third_step(0)
    second_step(1)
    compute(0)
    first_step(3)
    third_step(1)
    second_step(2)
    reduce_far(0)
    compute(1)
    third_step(2)
    second_step(3)
    reduce_near(0)
    reduce_far(1)
    compute(2)
    third_step(3)
    reduce_near(1)
    reduce_far(2)
    reduce_own(0)
    weight_grads(0)
    compute(3)
    reduce_near(2)
    reduce_own(1)
    reduce_far(3)
    reduce_own(2)
    reduce_near(3)
    weight_grads(1)
    store_in = pltpu.make_async_copy(st_in, gwin_hbm, o_sem.at[0])
    store_out = pltpu.make_async_copy(st_out, gwout_hbm, o_sem.at[1])
    store_in.start()
    store_out.start()
    reduce_own(3)

    @pl.loop(1, NZ * NX)
    def _(k):
        give_back(k).wait_recv()

    @pl.loop(1, NZ * NX)
    def _(k):
        a2a(k).wait_send()
        give_back(k).wait_send()

    for q in range(Q):
        for role in range(9):
            gather(q, role).wait_send()
        for j in range(NY):
            pair_sum(q, j).wait_send()
        for role in range(4):
            ring(q, role).wait_send()
    keep.wait()
    store_in.wait()
    store_out.wait()


def finish(ids_ref, gate_ref, home_hbm, gwin_in, gwout_in, gtok_ref, ggate_ref, gwin_hbm, gwout_hbm, home, sem):
    copies = [
        pltpu.make_async_copy(home_hbm, home, sem.at[0]),
        pltpu.make_async_copy(gwin_in, gwin_hbm, sem.at[1]),
        pltpu.make_async_copy(gwout_in, gwout_hbm, sem.at[2]),
    ]
    for copy in copies:
        copy.start()
    ex = lax.axis_index("expert")
    first, slot = places(ids_ref[...], ex // NX, ex % NX)
    first, slot = as_column(first).astype(I32), as_column(slot).astype(I32)
    gate = as_column(gate_ref[...])
    lanes = iota((T, NZ * NX * 16), 1)
    copies[0].wait()
    lines = home[...].reshape(NZ * NX * 16, BW)
    gtok_ref[:, 0:512] = mm(onehot(lanes == first + slot), lines).astype(BF)
    gtok_ref[:, 512:1024] = mm(onehot(lanes == first + 6 + slot), lines).astype(BF)
    low = jnp.where(slot < 3, first + 12 + slot, -1)
    high = jnp.where(slot < 3, -1, first + 9 + slot)
    gtok_ref[:, 1024:1280] = (
        mm(onehot(lanes == low), lines[:, 0:256]) + mm(onehot(lanes == high), lines[:, 256:512])
    ).astype(BF)
    gate_lines = mm(onehot(lanes == first + 15), lines[:, 0:128])
    gate_tok = jnp.sum(jnp.where(iota((T, 128), 1) == slot, gate_lines, 0.0), axis=1, keepdims=True) / gate
    ggate_ref[...] = jnp.broadcast_to(gate_tok, (T, T)).T[0:1, :].astype(BF)
    copies[1].wait()
    copies[2].wait()


def local(tokens, grad_out, gate, expert_ids, modality, modal_gain, w_in, w_out):
    vmem = pl.BlockSpec(memory_space=pltpu.VMEM)
    hbm = pl.BlockSpec(memory_space=pl.ANY)
    dma = pltpu.SemaphoreType.DMA
    gate_row, ids_row = gate.reshape(1, T), expert_ids.reshape(1, T)
    weights = [jax.ShapeDtypeStruct((D, F), BF), jax.ShapeDtypeStruct((F, D), BF)]
    home, in_part, out_part = pl.pallas_call(
        kernel,
        out_shape=[pltpu.VMEM((NZ * NX, 16, BW), BF), pltpu.VMEM((D, F), BF), pltpu.VMEM((F, D), BF)],
        in_specs=[vmem] * 6 + [hbm] * 2,
        out_specs=[hbm] * 3,
        scratch_shapes=[
            pltpu.VMEM((NZ * NX, 16, FW), BF),
            pltpu.VMEM((NZ * NX, 16, FW), BF),
            pltpu.VMEM((Q, 8, 2, RG, D), BF),
            pltpu.VMEM((D, F), BF),
            pltpu.VMEM((F, D), BF),
            pltpu.VMEM((M, F), F32),
            pltpu.VMEM((M, F), F32),
            pltpu.VMEM((Q, M, F), BF),
            pltpu.VMEM((Q, M, F), BF),
            pltpu.VMEM((Q, 8, 16, PW), BF),
            pltpu.VMEM((Q, NY, 16, PW), BF),
            pltpu.VMEM((Q, 2, 16, CUT), BF),
            pltpu.VMEM((Q, 2, 16, PW), BF),
            pltpu.VMEM((NZ * NX, 16, BW), BF),
            pltpu.VMEM((D, F), F32),
            pltpu.VMEM((F, D), F32),
            pltpu.VMEM((D, F), BF),
            pltpu.VMEM((F, D), BF),
            dma((3,)),
            dma((2,)),
            dma((NZ * NX,)),
            dma((NZ * NX,)),
            dma((Q, 9)),
            dma((Q, 9)),
            dma((Q, 8)),
            dma((Q, 8)),
            dma((NZ * NX,)),
            dma((NZ * NX,)),
        ],
        compiler_params=pltpu.CompilerParams(
            collective_id=0, has_side_effects=True, vmem_limit_bytes=56 * 1024 * 1024
        ),
        cost_estimate=pl.CostEstimate(flops=12_600_000_000, bytes_accessed=8_000_000, transcendentals=2_000_000),
    )(
        tokens,
        grad_out,
        gate_row,
        ids_row,
        modality.reshape(1, T),
        modal_gain,
        w_in[0],
        w_out[0],
    )
    grad_tokens, grad_gate, grad_in, grad_out_w = pl.pallas_call(
        finish,
        out_shape=[jax.ShapeDtypeStruct((T, D), BF), jax.ShapeDtypeStruct((1, T), BF)] + weights,
        in_specs=[vmem] * 2 + [hbm] * 3,
        out_specs=[vmem] * 2 + [hbm] * 2,
        scratch_shapes=[pltpu.VMEM((NZ * NX, 16, BW), BF), dma((3,))],
        compiler_params=pltpu.CompilerParams(vmem_limit_bytes=16 * 1024 * 1024),
    )(ids_row, gate_row, home, in_part, out_part)
    return grad_tokens, grad_gate.reshape(T), grad_in[None], grad_out_w[None]


def solution(mesh):
    rows = P(("dp", "expert"), None)
    flat = P(("dp", "expert"))
    return jax.shard_map(
        local,
        mesh=mesh,
        in_specs=(rows, rows, flat, rows, flat, P(), P("expert", None, "dp"), P("expert", "dp", None)),
        out_specs=(rows, flat, P("expert", None, "dp"), P("expert", "dp", None)),
        check_vma=False,
    )
```

```python
import functools

import jax
import jax.numpy as jnp
from jax import lax
from jax.experimental import pallas as pl
from jax.experimental.pallas import tpu as pltpu
from jax.sharding import PartitionSpec as P

MESH = pl.DeviceIdType.MESH
BF = jnp.bfloat16
F32 = jnp.float32
I32 = jnp.int32
ROOT = 0.7071067811865476
ROOT_PI = 0.3989422804014327

T, D, F, CAP = 128, 1280, 640, 6
NZ, NX, NY = 8, 4, 4
Q, GS = 4, 8
RG = GS * CAP
M = 8 * RG
FW, BW = 1024, 512
PW = 3 * D + 128
CUT = 2048


def iota(shape, dim):
    return lax.broadcasted_iota(I32, shape, dim)


def onehot(cond):
    return jnp.where(cond, 1.0, 0.0).astype(BF)


def mm(a, b):
    return jnp.dot(a, b, preferred_element_type=F32)


def mm_nt(a, b):
    return lax.dot_general(a, b, (((1,), (1,)), ((), ())), preferred_element_type=F32)


def mm_tn(a, b):
    return lax.dot_general(a, b, (((0,), (0,)), ((), ())), preferred_element_type=F32)


def sixth(v):
    return ((v.astype(F32) + 0.5) * (1.0 / 6.0)).astype(I32)


def offset(k):
    group = k // GS
    group += (group + 3) // 4 - 3 * (group // 3)
    pair = 2 * group + k // NX % 2
    far = (pair + 1) // 2
    return far * (2 * (pair % 2) - 1), k % NX


def as_column(row):
    return jnp.broadcast_to(row.astype(F32), (T, T)).T[:, 0:1]


def places(ids, z, x):
    wide = jnp.broadcast_to(ids.astype(F32), (T, T))
    same = (wide == wide.T) & (iota((T, T), 0) < iota((T, T), 1))
    slot = jnp.sum(jnp.where(same, 1.0, 0.0), axis=0, keepdims=True).astype(I32)
    dz = (z - (ids >> 2) + NZ) & (NZ - 1)
    pair = jnp.where(dz == 0, 0, jnp.where(dz <= NZ // 2, 2 * dz - 1, 2 * (NZ - dz)))
    group = pair >> 1
    group = jnp.where(group == 0, 0, jnp.where(group == 1, 3, group - 1))
    pair = 2 * group + (pair & 1)
    return (pair * NX + ((x - (ids & 3) + NX) & (NX - 1))) * 16, slot


def kernel(tok_ref, grad_ref, gate_ref, ids_ref, mod_ref, gain_ref, win_hbm, wout_hbm,
           home, gwin_hbm, gwout_hbm,
           out_buf, in_buf, rows, win, wout, pre, back, act16, pre16, part, sib, far, near, ret,
           acc_in, acc_out, st_in, st_out,
           w_sem, o_sem, as_sem, ar_sem, gs_sem, gr_sem, rs_sem, rr_sem, bs_sem, br_sem):
    dp, ex = lax.axis_index("dp"), lax.axis_index("expert")
    y, c = dp // 2, dp % 2
    z, x = ex // NX, ex % NX

    def column(step, core):
        return ((y + step + NY) % NY) * 2 + core

    up, down, other = {"dp": column(1, c)}, {"dp": column(-1, c)}, {"dp": y * 2 + 1 - c}

    def target(k):
        dz, dx = offset(k)
        return {"expert": ((z - dz + NZ) % NZ) * NX + (x - dx + NX) % NX}

    def source(k):
        dz, dx = offset(k)
        return {"expert": ((z + dz + NZ) % NZ) * NX + (x + dx) % NX}

    barrier = pltpu.get_barrier_semaphore()

    @pl.loop(1, NZ * NX)
    def _(k):
        pl.semaphore_signal(barrier, inc=1, device_id=target(k), device_id_type=MESH)

    for peer in (up, down, other):
        pl.semaphore_signal(barrier, inc=1, device_id=peer, device_id_type=MESH)

    load_in = pltpu.make_async_copy(win_hbm, win, w_sem.at[0])
    load_out = pltpu.make_async_copy(wout_hbm, wout, w_sem.at[1])
    load_in.start()
    load_out.start()

    def rdma(src, dst, ssem, rsem, dev):
        return pltpu.make_async_remote_copy(
            src_ref=src, dst_ref=dst, send_sem=ssem, recv_sem=rsem, device_id=dev, device_id_type=MESH
        )

    first, slot = places(ids_ref[...], z, x)
    gate_col = as_column(gate_ref[...])
    mod_col = as_column(mod_ref[...])
    gain = jnp.where(mod_col == 1.0, gain_ref[1:2, :], gain_ref[0:1, :])
    tok = tok_ref[...]
    gated = (gate_col * gain * grad_ref[...].astype(F32)).astype(BF)

    def tail(piece, j):
        return jnp.where((piece & 3) == j, first + 12 + (piece >> 2), -1)

    where_rows = [first + slot, first + 6 + slot]
    where_tail = [[tail(slot, j), tail(slot + 6, j)] for j in range(4)]

    def pack(q):
        lines = iota((GS * 16, T), 0) + q * GS * 16
        body = [onehot(lines == w) for w in where_rows]
        for j in range(4):
            lhs = jnp.concatenate(body + [onehot(lines == w) for w in where_tail[j]], axis=1)
            cols = slice(256 * j, 256 * j + 256)
            rhs = jnp.concatenate([tok[:, cols], gated[:, cols], tok[:, FW:], gated[:, FW:]], axis=0)
            out_buf[q * GS:(q + 1) * GS, :, cols] = mm(lhs, rhs).astype(BF).reshape(GS, 16, 256)

    def a2a(k):
        return rdma(out_buf.at[k], in_buf.at[k], as_sem.at[k], ar_sem.at[k], target(k))

    def dispatch(q):
        @pl.loop(max(1, q * GS), (q + 1) * GS)
        def _(k):
            a2a(k).start()

    for q in range(Q):
        pack(q)
        if q == 0:
            in_buf[0] = out_buf[0]
            pl.semaphore_wait(barrier, NZ * NX - 1 + 3)
        if q < 2:
            dispatch(q)

    cc = iota((1, GS * 16), 1)
    cs, ci = cc >> 4, cc & 15
    row_body = jnp.where(ci < 6, cs * 6 + ci, jnp.where(ci < 12, RG + cs * 6 + ci - 6, -1))

    def row_tail(j):
        p = (ci - 12) * 4 + j
        return jnp.where((ci >= 12) & (ci < 15), jnp.where(p < 6, cs * 6 + p, RG + cs * 6 + p - 6), -1)

    lines96 = iota((2 * RG, GS * 16), 0)
    un_body = onehot(lines96 == row_body)
    un_tail = jnp.concatenate([onehot(lines96 == row_tail(j)) for j in range(4)], axis=1)

    def gather(q, role):
        mine, below, above = dp, column(-1, c), column(1, c)
        beyond = column(2, c)
        d, half, dev = [
            (mine, None, up), (mine, None, down), (below, 0, up), (above, 1, down),
            (mine, None, other), (below, None, other), (above, None, other), (beyond, 0, other), (beyond, 1, other),
        ][role]
        ref = rows.at[q, d] if half is None else rows.at[q, d, half]
        return rdma(ref, ref, gs_sem.at[q, role], gr_sem.at[q, role], dev)

    def gather_wait(q, role):
        half = {2: 0, 3: 1, 7: 0, 8: 1}.get(role)
        d = {0: column(-1, c), 1: column(1, c), 2: column(2, c), 3: column(2, c), 4: column(0, 1 - c),
             5: column(-1, 1 - c), 6: column(1, 1 - c), 7: column(2, 1 - c), 8: column(2, 1 - c)}[role]
        ref = rows.at[q, d] if half is None else rows.at[q, d, half]
        rdma(ref, ref, gs_sem.at[q, role], gr_sem.at[q, role], other).wait_recv()

    def first_step(q):
        @pl.loop(max(1, q * GS), (q + 1) * GS)
        def _(k):
            a2a(k).wait_recv()

        got = in_buf[q * GS:(q + 1) * GS].reshape(GS * 16, FW)
        main = mm(un_body, got).astype(BF)
        stack = jnp.concatenate([got[:, 256 * j:256 * j + 256] for j in range(4)], axis=0)
        rest = mm(un_tail, stack).astype(BF)
        for h in range(2):
            rows[q, dp, h, :, 0:FW] = main[h * RG:(h + 1) * RG]
            rows[q, dp, h, :, FW:D] = rest[h * RG:(h + 1) * RG]
        for role in (0, 1, 4):
            gather(q, role).start()
        if q < 2:
            dispatch(q + 2)

    def second_step(q):
        gather_wait(q, 0)
        gather(q, 2).start()
        gather(q, 5).start()
        gather_wait(q, 1)
        gather(q, 3).start()
        gather(q, 6).start()

    def third_step(q):
        gather_wait(q, 2)
        gather(q, 7).start()
        gather_wait(q, 3)
        gather(q, 8).start()

    lane6 = iota((M, 128), 1)
    row_m = iota((M, 128), 0)
    gate_spread = lane6 == row_m - 6 * sixth(row_m)
    rr = iota((T, M), 0)
    gate_pick = onehot(((rr & 15) < 8) & (sixth(iota((T, M), 1)) == (rr >> 4) * 8 + (rr & 15)))

    def compute(q):
        for role in range(4, 9):
            gather_wait(q, role)
        if q == 0:
            load_in.wait()
            load_out.wait()
        pre[...] = mm(rows[q, :, 0].reshape(M, D), win[...])
        back[...] = mm_nt(rows[q, :, 1].reshape(M, D), wout[...])
        gates = []
        for r in range(0, M, 128):
            u = pre[r:r + 128]
            b = back[r:r + 128]
            cdf = 0.5 * (1.0 + lax.erf(u * ROOT))
            density = jnp.exp(-0.5 * u * u) * ROOT_PI
            act = u * cdf
            act16[q, r:r + 128] = act.astype(BF)
            pre16[q, r:r + 128] = (b * (cdf + u * density)).astype(BF)
            gates.append(jnp.sum(act * b, axis=1, keepdims=True))
        gate_sum = jnp.concatenate(gates, axis=0)
        spread = jnp.where(gate_spread, gate_sum, 0.0).astype(BF)
        part[q, :, :, 3 * D:PW] = mm(gate_pick, spread).astype(BF).reshape(8, 16, 128)
        tokens = mm_nt(pre16[q], win[...]).astype(BF).reshape(8, 3, 16, D)
        for g in range(3):
            part[q, :, :, g * D:(g + 1) * D] = tokens[:, g]
        for j in (2, 1, 3, 0):
            pair_sum(q, j).start()

    def pair_sum(q, j):
        return rdma(part.at[q, column(j, 1 - c)], sib.at[q, j], rs_sem.at[q, j], rr_sem.at[q, j], other)

    def ring(q, role):
        src, dst, dev = [
            (part.at[q, column(2, c), :, 0:CUT], far.at[q, 0, :, 0:CUT], up),
            (part.at[q, column(2, c), :, CUT:PW], far.at[q, 1, :, 0:PW - CUT], down),
            (part.at[q, column(1, c)], near.at[q, 0], up),
            (part.at[q, column(-1, c)], near.at[q, 1], down),
        ][role]
        return rdma(src, dst, rs_sem.at[q, 4 + role], rr_sem.at[q, 4 + role], dev)

    def add_pair(q, j):
        pair_sum(q, j).wait_recv()
        d = column(j, c)
        part[q, d] = (part[q, d].astype(F32) + sib[q, j].astype(F32)).astype(BF)

    def reduce_far(q):
        add_pair(q, 2)
        ring(q, 0).start()
        ring(q, 1).start()

    def reduce_near(q):
        add_pair(q, 1)
        ring(q, 0).wait_recv()
        d = column(1, c)
        part[q, d, :, 0:CUT] = (part[q, d, :, 0:CUT].astype(F32) + far[q, 0].astype(F32)).astype(BF)
        ring(q, 2).start()
        add_pair(q, 3)
        ring(q, 1).wait_recv()
        d = column(-1, c)
        part[q, d, :, CUT:PW] = (part[q, d, :, CUT:PW].astype(F32) + far[q, 1, :, 0:PW - CUT].astype(F32)).astype(BF)
        ring(q, 3).start()

    br = iota((GS * 16, 3 * RG), 0)
    bs, bi = br >> 4, br & 15
    bc = iota((GS * 16, 3 * RG), 1)

    def back_pick(h):
        return onehot(bc == jnp.where(bi < 6, bs * 6 + bi, jnp.where(
            bi < 12, RG + bs * 6 + bi - 6, jnp.where(bi < 15, 2 * RG + bs * 6 + bi - 12 + 3 * h, -1))))

    back_picks = [back_pick(0), back_pick(1)]
    gr = iota((GS * 16, 16), 0)
    gate_line = onehot(((gr & 15) == 15) & (iota((GS * 16, 16), 1) == (gr >> 4)))

    def give_back(k):
        return rdma(ret.at[k], home.at[k], bs_sem.at[k], br_sem.at[k], source(k))

    keep = pltpu.make_async_copy(ret.at[0], home.at[0], w_sem.at[2])

    def reduce_own(q):
        pair_sum(q, 0).wait_recv()
        total = part[q, dp].astype(F32) + sib[q, 0].astype(F32)
        ring(q, 2).wait_recv()
        ring(q, 3).wait_recv()
        total = (total + near[q, 0].astype(F32) + near[q, 1].astype(F32)).astype(BF)
        flat = jnp.concatenate([total[:, g * D:(g + 1) * D] for g in range(3)], axis=0)
        gates = mm(gate_line, total[:, 3 * D:PW])
        for h in range(2):
            rhs = jnp.concatenate(
                [flat[:, 256 * h:256 * h + 256], flat[:, 512 + 256 * h:768 + 256 * h], flat[:, 1024:1280]], axis=0
            )
            res = mm(back_picks[h], rhs)
            if h == 0:
                res = jnp.concatenate([res[:, 0:128] + gates, res[:, 128:256]], axis=1)
            ret[q * GS:(q + 1) * GS, :, 256 * h:256 * h + 256] = res.astype(BF).reshape(GS, 16, 256)
        if q == 0:
            keep.start()

        @pl.loop(max(1, q * GS), (q + 1) * GS)
        def _(k):
            give_back(k).start()

    def weight_grads(half):
        q0 = 2 * half
        a = act16[q0:q0 + 2].reshape(2 * M, F)
        p = pre16[q0:q0 + 2].reshape(2 * M, F)
        g_all = rows[q0:q0 + 2, :, 1].reshape(2 * M, D)
        x_all = rows[q0:q0 + 2, :, 0].reshape(2 * M, D)
        go = mm_tn(a, g_all)
        gi = mm_tn(x_all, p)
        if half == 0:
            acc_out[...] = go
            acc_in[...] = gi
        else:
            st_out[...] = (acc_out[...] + go).astype(BF)
            st_in[...] = (acc_in[...] + gi).astype(BF)

    first_step(0)
    first_step(1)
    second_step(0)
    first_step(2)
    third_step(0)
    second_step(1)
    compute(0)
    first_step(3)
    third_step(1)
    second_step(2)
    reduce_far(0)
    compute(1)
    second_step(3)
    third_step(2)
    reduce_near(0)
    reduce_far(1)
    compute(2)
    third_step(3)
    reduce_far(2)
    compute(3)
    reduce_near(1)
    reduce_far(3)
    reduce_own(0)
    reduce_near(2)
    weight_grads(0)
    reduce_own(1)
    reduce_near(3)
    weight_grads(1)
    store_in = pltpu.make_async_copy(st_in, gwin_hbm, o_sem.at[0])
    store_out = pltpu.make_async_copy(st_out, gwout_hbm, o_sem.at[1])
    store_in.start()
    store_out.start()
    reduce_own(2)
    reduce_own(3)

    @pl.loop(1, NZ * NX)
    def _(k):
        give_back(k).wait_recv()

    @pl.loop(1, NZ * NX)
    def _(k):
        a2a(k).wait_send()
        give_back(k).wait_send()

    for q in range(Q):
        for role in range(9):
            gather(q, role).wait_send()
        for j in range(NY):
            pair_sum(q, j).wait_send()
        for role in range(4):
            ring(q, role).wait_send()
    keep.wait()
    store_in.wait()
    store_out.wait()


def finish(ids_ref, gate_ref, home_hbm, gwin_in, gwout_in, gtok_ref, ggate_ref, gwin_hbm, gwout_hbm, home, sem):
    copies = [
        pltpu.make_async_copy(home_hbm, home, sem.at[0]),
        pltpu.make_async_copy(gwin_in, gwin_hbm, sem.at[1]),
        pltpu.make_async_copy(gwout_in, gwout_hbm, sem.at[2]),
    ]
    for copy in copies:
        copy.start()
    ex = lax.axis_index("expert")
    first, slot = places(ids_ref[...], ex // NX, ex % NX)
    first, slot = as_column(first).astype(I32), as_column(slot).astype(I32)
    gate = as_column(gate_ref[...])
    lanes = iota((T, NZ * NX * 16), 1)
    copies[0].wait()
    lines = home[...].reshape(NZ * NX * 16, BW)
    gtok_ref[:, 0:512] = mm(onehot(lanes == first + slot), lines).astype(BF)
    gtok_ref[:, 512:1024] = mm(onehot(lanes == first + 6 + slot), lines).astype(BF)
    low = jnp.where(slot < 3, first + 12 + slot, -1)
    high = jnp.where(slot < 3, -1, first + 9 + slot)
    gtok_ref[:, 1024:1280] = (
        mm(onehot(lanes == low), lines[:, 0:256]) + mm(onehot(lanes == high), lines[:, 256:512])
    ).astype(BF)
    gate_lines = mm(onehot(lanes == first + 15), lines[:, 0:128])
    gate_tok = jnp.sum(jnp.where(iota((T, 128), 1) == slot, gate_lines, 0.0), axis=1, keepdims=True) / gate
    ggate_ref[...] = jnp.broadcast_to(gate_tok, (T, T)).T[0:1, :].astype(BF)
    copies[1].wait()
    copies[2].wait()


def local(tokens, grad_out, gate, expert_ids, modality, modal_gain, w_in, w_out):
    vmem = pl.BlockSpec(memory_space=pltpu.VMEM)
    hbm = pl.BlockSpec(memory_space=pl.ANY)
    dma = pltpu.SemaphoreType.DMA
    gate_row, ids_row = gate.reshape(1, T), expert_ids.reshape(1, T)
    weights = [jax.ShapeDtypeStruct((D, F), BF), jax.ShapeDtypeStruct((F, D), BF)]
    home, in_part, out_part = pl.pallas_call(
        kernel,
        out_shape=[pltpu.VMEM((NZ * NX, 16, BW), BF), pltpu.VMEM((D, F), BF), pltpu.VMEM((F, D), BF)],
        in_specs=[vmem] * 6 + [hbm] * 2,
        out_specs=[hbm] * 3,
        scratch_shapes=[
            pltpu.VMEM((NZ * NX, 16, FW), BF),
            pltpu.VMEM((NZ * NX, 16, FW), BF),
            pltpu.VMEM((Q, 8, 2, RG, D), BF),
            pltpu.VMEM((D, F), BF),
            pltpu.VMEM((F, D), BF),
            pltpu.VMEM((M, F), F32),
            pltpu.VMEM((M, F), F32),
            pltpu.VMEM((Q, M, F), BF),
            pltpu.VMEM((Q, M, F), BF),
            pltpu.VMEM((Q, 8, 16, PW), BF),
            pltpu.VMEM((Q, NY, 16, PW), BF),
            pltpu.VMEM((Q, 2, 16, CUT), BF),
            pltpu.VMEM((Q, 2, 16, PW), BF),
            pltpu.VMEM((NZ * NX, 16, BW), BF),
            pltpu.VMEM((D, F), F32),
            pltpu.VMEM((F, D), F32),
            pltpu.VMEM((D, F), BF),
            pltpu.VMEM((F, D), BF),
            dma((3,)),
            dma((2,)),
            dma((NZ * NX,)),
            dma((NZ * NX,)),
            dma((Q, 9)),
            dma((Q, 9)),
            dma((Q, 8)),
            dma((Q, 8)),
            dma((NZ * NX,)),
            dma((NZ * NX,)),
        ],
        compiler_params=pltpu.CompilerParams(
            collective_id=0, has_side_effects=True, vmem_limit_bytes=56 * 1024 * 1024
        ),
        cost_estimate=pl.CostEstimate(flops=12_600_000_000, bytes_accessed=8_000_000, transcendentals=2_000_000),
    )(
        tokens,
        grad_out,
        gate_row,
        ids_row,
        modality.reshape(1, T),
        modal_gain,
        w_in[0],
        w_out[0],
    )
    grad_tokens, grad_gate, grad_in, grad_out_w = pl.pallas_call(
        finish,
        out_shape=[jax.ShapeDtypeStruct((T, D), BF), jax.ShapeDtypeStruct((1, T), BF)] + weights,
        in_specs=[vmem] * 2 + [hbm] * 3,
        out_specs=[vmem] * 2 + [hbm] * 2,
        scratch_shapes=[pltpu.VMEM((NZ * NX, 16, BW), BF), dma((3,))],
        compiler_params=pltpu.CompilerParams(vmem_limit_bytes=16 * 1024 * 1024),
    )(ids_row, gate_row, home, in_part, out_part)
    return grad_tokens, grad_gate.reshape(T), grad_in[None], grad_out_w[None]


def solution(mesh):
    rows = P(("dp", "expert"), None)
    flat = P(("dp", "expert"))
    return jax.shard_map(
        local,
        mesh=mesh,
        in_specs=(rows, rows, flat, rows, flat, P(), P("expert", None, "dp"), P("expert", "dp", None)),
        out_specs=(rows, flat, P("expert", None, "dp"), P("expert", "dp", None)),
        check_vma=False,
    )
```

```python
import functools

import jax
import jax.numpy as jnp
from jax import lax
from jax.experimental import pallas as pl
from jax.experimental.pallas import tpu as pltpu
from jax.sharding import PartitionSpec as P

MESH = pl.DeviceIdType.MESH
BF = jnp.bfloat16
F32 = jnp.float32
I32 = jnp.int32
ROOT = 0.7071067811865476
ROOT_PI = 0.3989422804014327

T, D, F, CAP = 128, 1280, 640, 6
NZ, NX, NY = 8, 4, 4
Q, GS = 4, 8
RG = GS * CAP
M = 8 * RG
FW, BW = 1024, 512
PW = 3 * D + 128
CUT = 2048


def iota(shape, dim):
    return lax.broadcasted_iota(I32, shape, dim)


def onehot(cond):
    return jnp.where(cond, 1.0, 0.0).astype(BF)


def mm(a, b):
    return jnp.dot(a, b, preferred_element_type=F32)


def mm_nt(a, b):
    return lax.dot_general(a, b, (((1,), (1,)), ((), ())), preferred_element_type=F32)


def mm_tn(a, b):
    return lax.dot_general(a, b, (((0,), (0,)), ((), ())), preferred_element_type=F32)


def sixth(v):
    return ((v.astype(F32) + 0.5) * (1.0 / 6.0)).astype(I32)


def offset(k):
    group = k // GS
    group += (group + 3) // 4 - 3 * (group // 3)
    pair = 2 * group + k // NX % 2
    far = (pair + 1) // 2
    return far * (2 * (pair % 2) - 1), k % NX


def as_column(row):
    return jnp.broadcast_to(row.astype(F32), (T, T)).T[:, 0:1]


def places(ids, z, x):
    wide = jnp.broadcast_to(ids.astype(F32), (T, T))
    same = (wide == wide.T) & (iota((T, T), 0) < iota((T, T), 1))
    slot = jnp.sum(jnp.where(same, 1.0, 0.0), axis=0, keepdims=True).astype(I32)
    dz = (z - (ids >> 2) + NZ) & (NZ - 1)
    pair = jnp.where(dz == 0, 0, jnp.where(dz <= NZ // 2, 2 * dz - 1, 2 * (NZ - dz)))
    group = pair >> 1
    group = jnp.where(group == 0, 0, jnp.where(group == 1, 3, group - 1))
    pair = 2 * group + (pair & 1)
    return (pair * NX + ((x - (ids & 3) + NX) & (NX - 1))) * 16, slot


def kernel(tok_ref, grad_ref, gate_ref, ids_ref, mod_ref, gain_ref, win_hbm, wout_hbm,
           home, gwin_hbm, gwout_hbm,
           out_buf, in_buf, rows, win, wout, pre, back, act16, pre16, part, sib, far, near, ret,
           acc_in, acc_out, st_in, st_out,
           w_sem, o_sem, as_sem, ar_sem, gs_sem, gr_sem, rs_sem, rr_sem, bs_sem, br_sem):
    dp, ex = lax.axis_index("dp"), lax.axis_index("expert")
    y, c = dp // 2, dp % 2
    z, x = ex // NX, ex % NX

    def column(step, core):
        return ((y + step + NY) % NY) * 2 + core

    up, down, other = {"dp": column(1, c)}, {"dp": column(-1, c)}, {"dp": y * 2 + 1 - c}

    def target(k):
        dz, dx = offset(k)
        return {"expert": ((z - dz + NZ) % NZ) * NX + (x - dx + NX) % NX}

    def source(k):
        dz, dx = offset(k)
        return {"expert": ((z + dz + NZ) % NZ) * NX + (x + dx) % NX}

    barrier = pltpu.get_barrier_semaphore()

    @pl.loop(1, NZ * NX)
    def _(k):
        pl.semaphore_signal(barrier, inc=1, device_id=target(k), device_id_type=MESH)

    for peer in (up, down, other):
        pl.semaphore_signal(barrier, inc=1, device_id=peer, device_id_type=MESH)

    load_in = pltpu.make_async_copy(win_hbm, win, w_sem.at[0])
    load_out = pltpu.make_async_copy(wout_hbm, wout, w_sem.at[1])
    load_in.start()
    load_out.start()

    def rdma(src, dst, ssem, rsem, dev):
        return pltpu.make_async_remote_copy(
            src_ref=src, dst_ref=dst, send_sem=ssem, recv_sem=rsem, device_id=dev, device_id_type=MESH
        )

    first, slot = places(ids_ref[...], z, x)
    gate_col = as_column(gate_ref[...])
    mod_col = as_column(mod_ref[...])
    gain = jnp.where(mod_col == 1.0, gain_ref[1:2, :], gain_ref[0:1, :])
    tok = tok_ref[...]
    gated = (gate_col * gain * grad_ref[...].astype(F32)).astype(BF)

    def tail(piece, j):
        return jnp.where((piece & 3) == j, first + 12 + (piece >> 2), -1)

    where_rows = [first + slot, first + 6 + slot]
    where_tail = [[tail(slot, j), tail(slot + 6, j)] for j in range(4)]

    def pack(q):
        lines = iota((GS * 16, T), 0) + q * GS * 16
        body = [onehot(lines == w) for w in where_rows]
        for j in range(4):
            lhs = jnp.concatenate(body + [onehot(lines == w) for w in where_tail[j]], axis=1)
            cols = slice(256 * j, 256 * j + 256)
            rhs = jnp.concatenate([tok[:, cols], gated[:, cols], tok[:, FW:], gated[:, FW:]], axis=0)
            out_buf[q * GS:(q + 1) * GS, :, cols] = mm(lhs, rhs).astype(BF).reshape(GS, 16, 256)

    def a2a(k):
        return rdma(out_buf.at[k], in_buf.at[k], as_sem.at[k], ar_sem.at[k], target(k))

    def dispatch(q):
        @pl.loop(max(1, q * GS), (q + 1) * GS)
        def _(k):
            a2a(k).start()

    for q in range(Q):
        pack(q)
        if q == 0:
            in_buf[0] = out_buf[0]
            pl.semaphore_wait(barrier, NZ * NX - 1 + 3)
        if q < 2:
            dispatch(q)

    cc = iota((1, GS * 16), 1)
    cs, ci = cc >> 4, cc & 15
    row_body = jnp.where(ci < 6, cs * 6 + ci, jnp.where(ci < 12, RG + cs * 6 + ci - 6, -1))

    def row_tail(j):
        p = (ci - 12) * 4 + j
        return jnp.where((ci >= 12) & (ci < 15), jnp.where(p < 6, cs * 6 + p, RG + cs * 6 + p - 6), -1)

    lines96 = iota((2 * RG, GS * 16), 0)
    un_body = onehot(lines96 == row_body)
    un_tail = jnp.concatenate([onehot(lines96 == row_tail(j)) for j in range(4)], axis=1)

    def gather(q, role):
        mine, below, above = dp, column(-1, c), column(1, c)
        beyond = column(2, c)
        d, half, dev = [
            (mine, None, up), (mine, None, down), (below, 0, up), (above, 1, down),
            (mine, None, other), (below, None, other), (above, None, other), (beyond, 0, other), (beyond, 1, other),
        ][role]
        ref = rows.at[q, d] if half is None else rows.at[q, d, half]
        return rdma(ref, ref, gs_sem.at[q, role], gr_sem.at[q, role], dev)

    def gather_wait(q, role):
        half = {2: 0, 3: 1, 7: 0, 8: 1}.get(role)
        d = {0: column(-1, c), 1: column(1, c), 2: column(2, c), 3: column(2, c), 4: column(0, 1 - c),
             5: column(-1, 1 - c), 6: column(1, 1 - c), 7: column(2, 1 - c), 8: column(2, 1 - c)}[role]
        ref = rows.at[q, d] if half is None else rows.at[q, d, half]
        rdma(ref, ref, gs_sem.at[q, role], gr_sem.at[q, role], other).wait_recv()

    def first_step(q):
        @pl.loop(max(1, q * GS), (q + 1) * GS)
        def _(k):
            a2a(k).wait_recv()

        got = in_buf[q * GS:(q + 1) * GS].reshape(GS * 16, FW)
        main = mm(un_body, got).astype(BF)
        stack = jnp.concatenate([got[:, 256 * j:256 * j + 256] for j in range(4)], axis=0)
        rest = mm(un_tail, stack).astype(BF)
        for h in range(2):
            rows[q, dp, h, :, 0:FW] = main[h * RG:(h + 1) * RG]
            rows[q, dp, h, :, FW:D] = rest[h * RG:(h + 1) * RG]
        for role in (0, 1, 4):
            gather(q, role).start()
        if q < 2:
            dispatch(q + 2)

    def second_step(q):
        gather_wait(q, 0)
        gather(q, 2).start()
        gather(q, 5).start()
        gather_wait(q, 1)
        gather(q, 3).start()
        gather(q, 6).start()

    def third_step(q):
        gather_wait(q, 2)
        gather(q, 7).start()
        gather_wait(q, 3)
        gather(q, 8).start()

    lane6 = iota((M, 128), 1)
    row_m = iota((M, 128), 0)
    gate_spread = lane6 == row_m - 6 * sixth(row_m)
    rr = iota((T, M), 0)
    gate_pick = onehot(((rr & 15) < 8) & (sixth(iota((T, M), 1)) == (rr >> 4) * 8 + (rr & 15)))

    def compute(q):
        for role in range(4, 9):
            gather_wait(q, role)
        if q == 0:
            load_in.wait()
            load_out.wait()
        pre[...] = mm(rows[q, :, 0].reshape(M, D), win[...])
        back[...] = mm_nt(rows[q, :, 1].reshape(M, D), wout[...])
        gates = []
        for r in range(0, M, 128):
            u = pre[r:r + 128]
            b = back[r:r + 128]
            cdf = 0.5 * (1.0 + lax.erf(u * ROOT))
            density = jnp.exp(-0.5 * u * u) * ROOT_PI
            act = u * cdf
            act16[q, r:r + 128] = act.astype(BF)
            pre16[q, r:r + 128] = (b * (cdf + u * density)).astype(BF)
            gates.append(jnp.sum(act * b, axis=1, keepdims=True))
        gate_sum = jnp.concatenate(gates, axis=0)
        spread = jnp.where(gate_spread, gate_sum, 0.0).astype(BF)
        part[q, :, :, 3 * D:PW] = mm(gate_pick, spread).astype(BF).reshape(8, 16, 128)
        tokens = mm_nt(pre16[q], win[...]).astype(BF).reshape(8, 3, 16, D)
        for g in range(3):
            part[q, :, :, g * D:(g + 1) * D] = tokens[:, g]
        for j in (2, 1, 3, 0):
            pair_sum(q, j).start()

    def pair_sum(q, j):
        return rdma(part.at[q, column(j, 1 - c)], sib.at[q, j], rs_sem.at[q, j], rr_sem.at[q, j], other)

    def ring(q, role):
        src, dst, dev = [
            (part.at[q, column(2, c), :, 0:CUT], far.at[q, 0, :, 0:CUT], up),
            (part.at[q, column(2, c), :, CUT:PW], far.at[q, 1, :, 0:PW - CUT], down),
            (part.at[q, column(1, c)], near.at[q, 0], up),
            (part.at[q, column(-1, c)], near.at[q, 1], down),
        ][role]
        return rdma(src, dst, rs_sem.at[q, 4 + role], rr_sem.at[q, 4 + role], dev)

    def add_pair(q, j):
        pair_sum(q, j).wait_recv()
        d = column(j, c)
        part[q, d] = (part[q, d].astype(F32) + sib[q, j].astype(F32)).astype(BF)

    def reduce_far(q):
        add_pair(q, 2)
        ring(q, 0).start()
        ring(q, 1).start()

    def reduce_near(q):
        add_pair(q, 1)
        ring(q, 0).wait_recv()
        d = column(1, c)
        part[q, d, :, 0:CUT] = (part[q, d, :, 0:CUT].astype(F32) + far[q, 0].astype(F32)).astype(BF)
        ring(q, 2).start()
        add_pair(q, 3)
        ring(q, 1).wait_recv()
        d = column(-1, c)
        part[q, d, :, CUT:PW] = (part[q, d, :, CUT:PW].astype(F32) + far[q, 1, :, 0:PW - CUT].astype(F32)).astype(BF)
        ring(q, 3).start()

    br = iota((GS * 16, 3 * RG), 0)
    bs, bi = br >> 4, br & 15
    bc = iota((GS * 16, 3 * RG), 1)

    def back_pick(h):
        return onehot(bc == jnp.where(bi < 6, bs * 6 + bi, jnp.where(
            bi < 12, RG + bs * 6 + bi - 6, jnp.where(bi < 15, 2 * RG + bs * 6 + bi - 12 + 3 * h, -1))))

    back_picks = [back_pick(0), back_pick(1)]
    gr = iota((GS * 16, 16), 0)
    gate_line = onehot(((gr & 15) == 15) & (iota((GS * 16, 16), 1) == (gr >> 4)))

    def give_back(k):
        return rdma(ret.at[k], home.at[k], bs_sem.at[k], br_sem.at[k], source(k))

    keep = pltpu.make_async_copy(ret.at[0], home.at[0], w_sem.at[2])

    def reduce_own(q):
        pair_sum(q, 0).wait_recv()
        total = part[q, dp].astype(F32) + sib[q, 0].astype(F32)
        ring(q, 2).wait_recv()
        ring(q, 3).wait_recv()
        total = (total + near[q, 0].astype(F32) + near[q, 1].astype(F32)).astype(BF)
        flat = jnp.concatenate([total[:, g * D:(g + 1) * D] for g in range(3)], axis=0)
        gates = mm(gate_line, total[:, 3 * D:PW])
        for h in range(2):
            rhs = jnp.concatenate(
                [flat[:, 256 * h:256 * h + 256], flat[:, 512 + 256 * h:768 + 256 * h], flat[:, 1024:1280]], axis=0
            )
            res = mm(back_picks[h], rhs)
            if h == 0:
                res = jnp.concatenate([res[:, 0:128] + gates, res[:, 128:256]], axis=1)
            ret[q * GS:(q + 1) * GS, :, 256 * h:256 * h + 256] = res.astype(BF).reshape(GS, 16, 256)
        if q == 0:
            keep.start()

        @pl.loop(max(1, q * GS), (q + 1) * GS)
        def _(k):
            give_back(k).start()

    def weight_grads(half):
        q0 = 2 * half
        a = act16[q0:q0 + 2].reshape(2 * M, F)
        p = pre16[q0:q0 + 2].reshape(2 * M, F)
        g_all = rows[q0:q0 + 2, :, 1].reshape(2 * M, D)
        x_all = rows[q0:q0 + 2, :, 0].reshape(2 * M, D)
        go = mm_tn(a, g_all)
        gi = mm_tn(x_all, p)
        if half == 0:
            acc_out[...] = go
            acc_in[...] = gi
        else:
            st_out[...] = (acc_out[...] + go).astype(BF)
            st_in[...] = (acc_in[...] + gi).astype(BF)

    first_step(0)
    first_step(1)
    second_step(0)
    first_step(2)
    third_step(0)
    second_step(1)
    compute(0)
    first_step(3)
    third_step(1)
    second_step(2)
    reduce_far(0)
    compute(1)
    second_step(3)
    third_step(2)
    reduce_near(0)
    reduce_far(1)
    compute(2)
    third_step(3)
    reduce_far(2)
    compute(3)
    reduce_near(1)
    reduce_far(3)
    reduce_own(0)
    reduce_near(2)
    weight_grads(0)
    reduce_own(1)
    reduce_near(3)
    reduce_own(2)
    weight_grads(1)
    store_in = pltpu.make_async_copy(st_in, gwin_hbm, o_sem.at[0])
    store_out = pltpu.make_async_copy(st_out, gwout_hbm, o_sem.at[1])
    store_in.start()
    store_out.start()
    reduce_own(3)

    @pl.loop(1, NZ * NX)
    def _(k):
        give_back(k).wait_recv()

    @pl.loop(1, NZ * NX)
    def _(k):
        a2a(k).wait_send()
        give_back(k).wait_send()

    for q in range(Q):
        for role in range(9):
            gather(q, role).wait_send()
        for j in range(NY):
            pair_sum(q, j).wait_send()
        for role in range(4):
            ring(q, role).wait_send()
    keep.wait()
    store_in.wait()
    store_out.wait()


def finish(ids_ref, gate_ref, home_hbm, gwin_in, gwout_in, gtok_ref, ggate_ref, gwin_hbm, gwout_hbm, home, sem):
    copies = [
        pltpu.make_async_copy(home_hbm, home, sem.at[0]),
        pltpu.make_async_copy(gwin_in, gwin_hbm, sem.at[1]),
        pltpu.make_async_copy(gwout_in, gwout_hbm, sem.at[2]),
    ]
    for copy in copies:
        copy.start()
    ex = lax.axis_index("expert")
    first, slot = places(ids_ref[...], ex // NX, ex % NX)
    first, slot = as_column(first).astype(I32), as_column(slot).astype(I32)
    gate = as_column(gate_ref[...])
    lanes = iota((T, NZ * NX * 16), 1)
    copies[0].wait()
    lines = home[...].reshape(NZ * NX * 16, BW)
    gtok_ref[:, 0:512] = mm(onehot(lanes == first + slot), lines).astype(BF)
    gtok_ref[:, 512:1024] = mm(onehot(lanes == first + 6 + slot), lines).astype(BF)
    low = jnp.where(slot < 3, first + 12 + slot, -1)
    high = jnp.where(slot < 3, -1, first + 9 + slot)
    gtok_ref[:, 1024:1280] = (
        mm(onehot(lanes == low), lines[:, 0:256]) + mm(onehot(lanes == high), lines[:, 256:512])
    ).astype(BF)
    gate_lines = mm(onehot(lanes == first + 15), lines[:, 0:128])
    gate_tok = jnp.sum(jnp.where(iota((T, 128), 1) == slot, gate_lines, 0.0), axis=1, keepdims=True) / gate
    ggate_ref[...] = jnp.broadcast_to(gate_tok, (T, T)).T[0:1, :].astype(BF)
    copies[1].wait()
    copies[2].wait()


def local(tokens, grad_out, gate, expert_ids, modality, modal_gain, w_in, w_out):
    vmem = pl.BlockSpec(memory_space=pltpu.VMEM)
    hbm = pl.BlockSpec(memory_space=pl.ANY)
    dma = pltpu.SemaphoreType.DMA
    gate_row, ids_row = gate.reshape(1, T), expert_ids.reshape(1, T)
    weights = [jax.ShapeDtypeStruct((D, F), BF), jax.ShapeDtypeStruct((F, D), BF)]
    home, in_part, out_part = pl.pallas_call(
        kernel,
        out_shape=[pltpu.VMEM((NZ * NX, 16, BW), BF), pltpu.VMEM((D, F), BF), pltpu.VMEM((F, D), BF)],
        in_specs=[vmem] * 6 + [hbm] * 2,
        out_specs=[hbm] * 3,
        scratch_shapes=[
            pltpu.VMEM((NZ * NX, 16, FW), BF),
            pltpu.VMEM((NZ * NX, 16, FW), BF),
            pltpu.VMEM((Q, 8, 2, RG, D), BF),
            pltpu.VMEM((D, F), BF),
            pltpu.VMEM((F, D), BF),
            pltpu.VMEM((M, F), F32),
            pltpu.VMEM((M, F), F32),
            pltpu.VMEM((Q, M, F), BF),
            pltpu.VMEM((Q, M, F), BF),
            pltpu.VMEM((Q, 8, 16, PW), BF),
            pltpu.VMEM((Q, NY, 16, PW), BF),
            pltpu.VMEM((Q, 2, 16, CUT), BF),
            pltpu.VMEM((Q, 2, 16, PW), BF),
            pltpu.VMEM((NZ * NX, 16, BW), BF),
            pltpu.VMEM((D, F), F32),
            pltpu.VMEM((F, D), F32),
            pltpu.VMEM((D, F), BF),
            pltpu.VMEM((F, D), BF),
            dma((3,)),
            dma((2,)),
            dma((NZ * NX,)),
            dma((NZ * NX,)),
            dma((Q, 9)),
            dma((Q, 9)),
            dma((Q, 8)),
            dma((Q, 8)),
            dma((NZ * NX,)),
            dma((NZ * NX,)),
        ],
        compiler_params=pltpu.CompilerParams(
            collective_id=0, has_side_effects=True, vmem_limit_bytes=56 * 1024 * 1024
        ),
        cost_estimate=pl.CostEstimate(flops=12_600_000_000, bytes_accessed=8_000_000, transcendentals=2_000_000),
    )(
        tokens,
        grad_out,
        gate_row,
        ids_row,
        modality.reshape(1, T),
        modal_gain,
        w_in[0],
        w_out[0],
    )
    grad_tokens, grad_gate, grad_in, grad_out_w = pl.pallas_call(
        finish,
        out_shape=[jax.ShapeDtypeStruct((T, D), BF), jax.ShapeDtypeStruct((1, T), BF)] + weights,
        in_specs=[vmem] * 2 + [hbm] * 3,
        out_specs=[vmem] * 2 + [hbm] * 2,
        scratch_shapes=[pltpu.VMEM((NZ * NX, 16, BW), BF), dma((3,))],
        compiler_params=pltpu.CompilerParams(vmem_limit_bytes=16 * 1024 * 1024),
    )(ids_row, gate_row, home, in_part, out_part)
    return grad_tokens, grad_gate.reshape(T), grad_in[None], grad_out_w[None]


def solution(mesh):
    rows = P(("dp", "expert"), None)
    flat = P(("dp", "expert"))
    return jax.shard_map(
        local,
        mesh=mesh,
        in_specs=(rows, rows, flat, rows, flat, P(), P("expert", None, "dp"), P("expert", "dp", None)),
        out_specs=(rows, flat, P("expert", None, "dp"), P("expert", "dp", None)),
        check_vma=False,
    )
```
